32 devices in a mesh: seq: 8 (over z, x), head: 4 (over y, core).
Axes of the slice: x: 2, y: 2, z: 4, core: 2. Of those that a mesh axis runs over, the one named last changes fastest.
Arguments:
- queries: bfloat16 [1024, 4096], P(('seq', 'head')), may hold values from -6 to 6
- keys: bfloat16 [1024, 4096], P(('seq', 'head')), may hold values from -6 to 6
- values: bfloat16 [1024, 4096], P(('seq', 'head')), may hold values from -6 to 6
- grad_out: bfloat16 [1024, 4096], P(('seq', 'head')), may hold values from -6 to 6
- random_blocks: int32 [32, 16, 3], replicated, may hold values from 0 to 15, as said below
- global_blocks: int32 [2], replicated, may hold values from 0 to 15
Outputs:
- attended: bfloat16 [1024, 4096], P(('seq', 'head'))
- grad_queries: bfloat16 [1024, 4096], P(('seq', 'head'))
- grad_keys: bfloat16 [1024, 4096], P(('seq', 'head'))
- grad_values: bfloat16 [1024, 4096], P(('seq', 'head'))
The draws below stay inside these ranges and needn't reach their ends.
Inputs may be any that keep to these rules, and one draw needn't show every extreme that they name: `random_blocks`: for the heads of one index of head and the query blocks of one index of seq, at most 7 random entries lie in the blocks of any one index of seq, and in every such group some index of seq holds exactly 7.
All inputs are finite; a program needn't handle non-finite values.
Results may differ from the reference program's by a relative error of at most 0.034.
Values may be sent and summed in bfloat16 or wider, within the bound.
No kernel may reach another device: no remote copies, remote signals or barrier semaphores. Data moves between devices by JAX's collectives and lax.ppermute only.
A program may use at most 128 MiB of HBM per device.

```python
import jax
import jax.numpy as jnp
from jax import lax

HEADS = 32
HEAD_DIM = 128
BLOCK = 64
RAND_BLOCKS = 3
GLOB_BLOCKS = 2
SEQ_LEN = 1024
BLOCKS = 16
QBLK_DEV = 2
SEQ_SHARDS = 8
HEADS_DEV = 8
REQUESTS = 48
SLOTS = 7


def draw_queries(key, part):
    shape = (SEQ_LEN, HEADS * HEAD_DIM)
    filled = jax.random.truncated_normal(jax.random.fold_in(key, 11), -6.0, 6.0, shape, jnp.float32)
    return filled.astype(jnp.bfloat16)


def draw_keys(key, part):
    shape = (SEQ_LEN, HEADS * HEAD_DIM)
    filled = jax.random.truncated_normal(jax.random.fold_in(key, 12), -6.0, 6.0, shape, jnp.float32)
    return filled.astype(jnp.bfloat16)


def draw_random_blocks(key, part):
    groups = HEADS // HEADS_DEV
    pool_size = SEQ_SHARDS * SLOTS

    def draw_group(group_id):
        group_key = jax.random.fold_in(jax.random.fold_in(key, 31), group_id)
        first, second, third, fourth = jax.random.split(group_key, 4)
        busiest = jax.random.randint(first, (), 0, SEQ_SHARDS)
        holder = jnp.arange(pool_size, dtype=jnp.int32) // SLOTS
        ranking = jax.random.permutation(second, pool_size).astype(jnp.int32)
        ranking = jnp.where(holder == busiest, -1 - jnp.arange(pool_size, dtype=jnp.int32), ranking)
        picked = holder[jnp.argsort(ranking)[:REQUESTS]]
        picked = picked[jax.random.permutation(third, REQUESTS)]
        offset = jax.random.randint(fourth, (REQUESTS,), 0, QBLK_DEV)
        return picked * QBLK_DEV + offset
    drawn = jax.vmap(draw_group)(jnp.arange(groups * SEQ_SHARDS, dtype=jnp.int32))
    drawn = drawn.reshape(groups, SEQ_SHARDS, HEADS_DEV, QBLK_DEV, RAND_BLOCKS).transpose(0, 2, 1, 3, 4)
    return drawn.reshape(HEADS, BLOCKS, RAND_BLOCKS).astype(jnp.int32)


def block_scale(key, extent, pieces, least, largest):
    def one(position, blocks):
        heights = jax.random.uniform(jax.random.fold_in(jax.random.fold_in(key, 6), position), (blocks,), jnp.float32, least / len(pieces), largest / len(pieces))
        return jnp.repeat(jnp.exp(heights), extent[position] // blocks).reshape((-1,) + (1,) * (len(extent) - position - 1))

    loudness = one(*pieces[0])
    for cut in pieces[1:]:
        loudness = loudness * one(*cut)
    return loudness


def scatter_about(rng, extent, width, reach, cuts=(), held_as=jnp.bfloat16):
    values = jax.random.normal(rng, extent, jnp.float32) * width
    if len(cuts) > 0:
        values = block_scale(rng, extent, cuts, -0.22, 0.18) * values
    return jnp.clip(values, min=-reach, max=reach).astype(held_as)


def setup_inputs(seed: int = 0) -> dict:
    seeds = jax.random.split(jax.random.key(seed), 7)
    return {
        "queries": draw_queries(jax.random.fold_in(seeds[6], 71), 0),
        "keys": draw_keys(jax.random.fold_in(seeds[6], 71), 0),
        "values": scatter_about(seeds[2], (SEQ_LEN, HEADS * HEAD_DIM), 1.0, 6.0, ((0, 32),)),
        "grad_out": scatter_about(seeds[3], (SEQ_LEN, HEADS * HEAD_DIM), 1.0, 6.0, ((0, 32),)),
        "random_blocks": draw_random_blocks(jax.random.fold_in(seeds[6], 71), 0),
        "global_blocks": jax.random.randint(seeds[5], (GLOB_BLOCKS,), 0, BLOCKS).astype(jnp.int32),
    }


def reference(queries, keys, values, grad_out, random_blocks, global_blocks):
    score_scale = HEAD_DIM ** -0.5
    block_index = jnp.arange(BLOCKS, dtype=jnp.int32)
    split_at = 3 + GLOB_BLOCKS

    def one_head(head_id):
        def head_slice(array):
            return lax.dynamic_slice_in_dim(array, head_id * HEAD_DIM, HEAD_DIM, 1).reshape(BLOCKS, BLOCK, HEAD_DIM)

        query_float = head_slice(queries).astype(jnp.float32)
        key_rows = head_slice(keys)
        value_rows = head_slice(values)
        incoming_gradient = head_slice(grad_out).astype(jnp.float32)
        rand_list = lax.dynamic_index_in_dim(random_blocks, head_id, 0, keepdims=False).astype(jnp.int32)
        window_list = jnp.stack([block_index - 1, block_index, block_index + 1], axis=1)
        glob_list = jnp.broadcast_to(global_blocks[None, :].astype(jnp.int32), (BLOCKS, GLOB_BLOCKS))
        key_index = jnp.concatenate([window_list, glob_list, rand_list], axis=1)
        key_valid = jnp.concatenate([jnp.stack([block_index >= 1, block_index >= 0, block_index + 1 < BLOCKS], axis=1), jnp.ones((BLOCKS, GLOB_BLOCKS + RAND_BLOCKS), bool)], axis=1)
        clipped = jnp.clip(key_index, 0, BLOCKS - 1)
        key_blocks_gathered = key_rows[clipped].astype(jnp.float32)
        value_blocks_gathered = value_rows[clipped].astype(jnp.float32)
        attention_logits = jnp.einsum("cmp,clqp->cmlq", query_float, key_blocks_gathered) * score_scale
        attention_logits = jnp.where(key_valid[:, None, :, None], attention_logits, -jnp.inf)
        row_max = jnp.max(attention_logits, axis=(2, 3), keepdims=True)
        exponent = jnp.exp(attention_logits - row_max)
        row_sum = jnp.sum(exponent, axis=(2, 3), keepdims=True)
        probability = exponent / row_sum
        attention_weight = lax.optimization_barrier(probability.astype(jnp.bfloat16)).astype(jnp.float32)
        attended = jnp.einsum("qczt,qzth->qch", attention_weight, value_blocks_gathered).astype(jnp.bfloat16)
        row_delta = jnp.sum(incoming_gradient * attended.astype(jnp.float32), axis=2)
        probability_gradient = jnp.einsum("cmp,clqp->cmlq", incoming_gradient, value_blocks_gathered)
        logit_gradient = probability * (probability_gradient - row_delta[:, :, None, None])
        logit_gradient = lax.optimization_barrier(logit_gradient.astype(jnp.bfloat16)).astype(jnp.float32)
        query_gradient = (score_scale * jnp.einsum("qczt,qzth->qch", logit_gradient, key_blocks_gathered)).astype(jnp.bfloat16)
        key_contribution = score_scale * jnp.einsum("okrt,okp->ortp", logit_gradient, query_float)
        value_contribution = jnp.einsum("okrt,okp->ortp", attention_weight, incoming_gradient)

        def rounded_tail(term):
            tail = lax.optimization_barrier(term[:, split_at:].astype(jnp.bfloat16)).astype(jnp.float32)
            joined = jnp.concatenate([term[:, :split_at], tail], axis=1)
            return jnp.where(key_valid[:, :, None, None], joined, 0.0)

        empty = jnp.zeros((BLOCKS, BLOCK, HEAD_DIM), jnp.float32)
        grad_key = empty.at[clipped].add(rounded_tail(key_contribution)).astype(jnp.bfloat16)
        grad_value = empty.at[clipped].add(rounded_tail(value_contribution)).astype(jnp.bfloat16)
        return attended, query_gradient, grad_key, grad_value

    results = lax.map(one_head, jnp.arange(HEADS, dtype=jnp.int32))

    def to_rows(stacked):
        return stacked.transpose(1, 2, 0, 3).reshape(BLOCKS * BLOCK, HEADS * HEAD_DIM)

    return (to_rows(results[0]), to_rows(results[1]), to_rows(results[2]), to_rows(results[3]))
```

```python
import functools
import math

import jax
import jax.numpy as jnp
from jax import lax
from jax.experimental import pallas as pl
from jax.experimental.pallas import tpu as pltpu
from jax.sharding import Mesh
from jax.sharding import PartitionSpec as P

HEAD_DIM = 128
BLOCK = 64
SCALE = HEAD_DIM**-0.5
QUERY_TILE = 256
KEY_TILE = 512

WHOLE = pl.BlockSpec(memory_space=pltpu.VMEM)
FAR = pl.BlockSpec(memory_space=pltpu.HBM)


def dot(a, b):
    return lax.dot_general(a, b, (((1,), (0,)), ((), ())), preferred_element_type=jnp.float32)


def dot_nt(a, b):
    return lax.dot_general(a, b, (((1,), (1,)), ((), ())), preferred_element_type=jnp.float32)


def each(count, step, start):
    if count <= 4:
        carry = start
        for i in range(count):
            carry = step(i, carry)
        return carry
    return lax.fori_loop(0, count, step, start)


def copies(pairs, sems):
    made = [pltpu.make_async_copy(a, b, sems.at[i]) for i, (a, b) in enumerate(pairs)]
    for copy in made:
        copy.start()
    return made


def wait_all(made):
    for copy in made:
        copy.wait()


def pack_kernel(random_ref, global_ref, *refs):
    *ins, out, random_out, global_out, held, sems = refs
    pairs = [(x, held.at[a]) for a, x in enumerate(ins)]
    pairs += [(random_ref, random_out), (global_ref, global_out)]
    wait_all(copies(pairs, sems))
    for h in range(out.shape[0]):
        for a in range(len(ins)):
            out[h, a] = held[a, :, h * HEAD_DIM : (h + 1) * HEAD_DIM]


def pack(arrays, tables):
    rows, width = arrays[0].shape
    kind = arrays[0].dtype
    shape = (width // HEAD_DIM, len(arrays), rows, HEAD_DIM)
    ins = [pltpu.with_memory_space_constraint(x, pltpu.HBM) for x in tables + arrays]
    return pl.pallas_call(
        pack_kernel,
        out_shape=[pltpu.VMEM(shape, kind)] + [pltpu.VMEM(x.shape, x.dtype) for x in tables],
        in_specs=[FAR] * len(ins),
        out_specs=[WHOLE] * (1 + len(tables)),
        scratch_shapes=[
            pltpu.VMEM((len(arrays), rows, width), kind),
            pltpu.SemaphoreType.DMA((len(ins),)),
        ],
        compiler_params=pltpu.CompilerParams(vmem_limit_bytes=8 << 20),
    )(*ins)


def unpack_kernel(packed, *refs):
    outs, (held, sems) = refs[:-2], refs[-2:]
    leaving = []
    for a, out in enumerate(outs):
        for h in range(packed.shape[0]):
            held[a, :, h * HEAD_DIM : (h + 1) * HEAD_DIM] = packed[h, a]
        leaving.append(pltpu.make_async_copy(held.at[a], out, sems.at[a]))
        leaving[-1].start()
    wait_all(leaving)


def unpack(packed):
    heads, arrays, rows, depth = packed.shape
    return pl.pallas_call(
        unpack_kernel,
        out_shape=[jax.ShapeDtypeStruct((rows, heads * depth), packed.dtype)] * arrays,
        in_specs=[WHOLE],
        out_specs=[FAR] * arrays,
        scratch_shapes=[
            pltpu.VMEM((arrays, rows, heads * depth), packed.dtype),
            pltpu.SemaphoreType.DMA((arrays,)),
        ],
        compiler_params=pltpu.CompilerParams(vmem_limit_bytes=8 << 20),
    )(packed)


def tile_of(pair, start, size):
    ref, slot = pair
    rows = ref.shape[2]
    lanes = pl.ds(start // rows, size // rows)
    return ref[lanes, slot].reshape(size, HEAD_DIM)


def put(pair, start, tile):
    ref, slot = pair
    size, rows = tile.shape[0], ref.shape[2]
    lanes = pl.ds(start // rows, size // rows)
    ref[lanes, slot] = tile.astype(ref.dtype).reshape(size // rows, rows, HEAD_DIM)


def span(i, size):
    return pl.ds(pl.multiple_of(i * size, size), size)


def flip(pair, out, length):
    step = min(512, length)

    def one(i, _):
        tile = tile_of(pair, i * step, step)
        out[:HEAD_DIM, span(i, step)] = tile.astype(jnp.float32).T.astype(out.dtype)
        return 0

    each(length // step, one, 0)


def list_bias(random_ref, global_ref, bias_ref):
    steps, group, queries = bias_ref.shape
    blocks, total = queries // BLOCK, steps * group
    first = lax.axis_index("crew") * blocks
    shape = (blocks, total)
    names = lax.broadcasted_iota(jnp.int32, shape, 1)
    own = first + lax.broadcasted_iota(jnp.int32, shape, 0)
    times = (jnp.abs(names - own) <= 1).astype(jnp.float32)
    for i in range(global_ref.shape[1]):
        times += (names == global_ref[:, i : i + 1]).astype(jnp.float32)
    heads = random_ref.shape[2]
    mine = lax.broadcasted_iota(jnp.int32, (blocks, heads), 1) == lax.axis_index("lane")
    for i in range(random_ref.shape[0]):
        picks = jnp.where(mine, random_ref[i, pl.ds(first, blocks), :], 0)
        times += (names == jnp.sum(picks, axis=1, keepdims=True)).astype(jnp.float32)
    place = lax.broadcasted_iota(jnp.int32, (blocks, queries), 1) // BLOCK
    place = (place == lax.broadcasted_iota(jnp.int32, (blocks, queries), 0)).astype(jnp.bfloat16)
    wide = lax.dot_general(
        times.astype(jnp.bfloat16), place, (((0,), (0,)), ((), ())), preferred_element_type=jnp.float32
    )
    bias = jnp.where(wide > 0.0, jnp.log2(jnp.maximum(wide, 1.0)), -jnp.inf)
    bias_ref[...] = bias.reshape(steps, group, queries)


def attend_kernel(
    q_at, g_at, k_at, v_at, random_ref, global_ref, out_at, dq_at, dk_at, dv_at,
    score_ref, w_ref, ds_ref, bias_ref, kt_ref, vt_ref, gt_ref, gs_ref, delta_ref,
):
    keys, queries = w_ref.shape
    steps = keys // KEY_TILE
    turns = queries // QUERY_TILE
    factor = SCALE * math.log2(math.e)
    list_bias(random_ref, global_ref, bias_ref)
    flip(v_at, vt_ref, keys)
    vt_ref[HEAD_DIM:, :] = jnp.ones_like(vt_ref[HEAD_DIM:, :])

    def through(left_ref, right_ref, here):
        def add(c, total):
            at = span(c, KEY_TILE)
            return total + dot(left_ref[:, at], right_ref[at, here])

        if steps <= 4:
            return dot(left_ref[...], right_ref[:, here])
        return each(steps, add, jnp.zeros((left_ref.shape[0], QUERY_TILE), jnp.float32))

    def blocks_of(x):
        return x.reshape(KEY_TILE // BLOCK, BLOCK, QUERY_TILE)

    def score(t):
        here = span(t, QUERY_TILE)
        held = score_ref.at[t % 2]
        q = tile_of(q_at, t * QUERY_TILE, QUERY_TILE)

        def one(c, top):
            raw = dot_nt(tile_of(k_at, c * KEY_TILE, KEY_TILE), q)
            held[span(c, KEY_TILE), :] = raw
            listed = jnp.where(bias_ref[c, :, here] > -jnp.inf, 0.0, -jnp.inf)
            best = jnp.max(blocks_of(raw), axis=1) + listed
            return jnp.maximum(top, jnp.max(best, axis=0, keepdims=True))

        return each(steps, one, jnp.full((1, QUERY_TILE), -jnp.inf, jnp.float32)) * factor

    def weigh(t, top):
        here = span(t, QUERY_TILE)
        held = score_ref.at[t % 2]

        def one(c, _):
            at = span(c, KEY_TILE)
            shift = bias_ref[c, :, here] - top
            e = jnp.exp2(blocks_of(held[at, :]) * factor + shift[:, None, :])
            w_ref[at, here] = e.reshape(KEY_TILE, QUERY_TILE).astype(w_ref.dtype)
            return 0

        each(steps, one, 0)

    def mix(t):
        here = span(t, QUERY_TILE)
        mixed = through(vt_ref, w_ref, here)
        inverse = 1.0 / mixed[HEAD_DIM : HEAD_DIM + 1]
        out = (mixed[:HEAD_DIM] * inverse).astype(jnp.bfloat16).astype(jnp.float32)
        put(out_at, t * QUERY_TILE, out.T)
        g = tile_of(g_at, t * QUERY_TILE, QUERY_TILE).astype(jnp.float32).T
        delta_ref[:, here] = jnp.sum(g * out, axis=0, keepdims=True) * inverse
        g = g * inverse
        gt_ref[:, here] = g.astype(gt_ref.dtype)
        gs_ref[here, :] = g.T.astype(gs_ref.dtype)

    tops = [score(0)]
    for t in range(turns):
        if t + 1 < turns:
            tops.append(score(t + 1))
        weigh(t, tops[t])
        mix(t)

    def backward(c, _):
        at = span(c, KEY_TILE)
        put(dv_at, c * KEY_TILE, dot(w_ref[at, :], gs_ref[...]))
        v = tile_of(v_at, c * KEY_TILE, KEY_TILE)
        for t in range(turns):
            here = span(t, QUERY_TILE)
            gap = dot(v, gt_ref[:, here]) - delta_ref[:, here]
            ds_ref[at, here] = (w_ref[at, here].astype(jnp.float32) * gap).astype(ds_ref.dtype)
        q = tile_of(q_at, 0, queries)
        put(dk_at, c * KEY_TILE, dot(ds_ref[at, :], q) * SCALE)
        return 0

    each(steps, backward, 0)
    flip(k_at, kt_ref, keys)
    for t in range(turns):
        put(dq_at, t * QUERY_TILE, (through(kt_ref, ds_ref, span(t, QUERY_TILE)) * SCALE).T)


def attend(rows, wide, random_blocks, global_blocks):
    team, _, height, _ = rows.shape
    queries = team * height
    apart = len(wide) > 0
    keys = wide[0].shape[0] * height if apart else queries
    outs = [jax.ShapeDtypeStruct((team, 2 if apart else 4, height, HEAD_DIM), rows.dtype)]
    if apart:
        outs += [jax.ShapeDtypeStruct(x.shape, jnp.float32) for x in wide]

    def kernel(*refs):
        rows_ref, *refs = refs
        k_at, v_at, dk_at, dv_at = (rows_ref, 2), (rows_ref, 3), None, None
        if apart:
            k_at, v_at, *refs = [(refs[0], 0), (refs[1], 0)] + refs[2:]
        random_ref, global_ref, out_ref, *refs = refs
        dk_at, dv_at = (out_ref, 2), (out_ref, 3)
        if apart:
            dk_at, dv_at, *refs = [(refs[0], 0), (refs[1], 0)] + refs[2:]
        score_ref, w_ref, *refs = refs
        ds_ref, *refs = [w_ref] + refs if apart else refs
        attend_kernel(
            (rows_ref, 0), (rows_ref, 1), k_at, v_at, random_ref, global_ref, (out_ref, 0), (out_ref, 1),
            dk_at, dv_at, score_ref, w_ref, ds_ref, *refs,
        )

    narrow = functools.partial(pltpu.VMEM, dtype=rows.dtype)
    ins = [rows, *wide, random_blocks, global_blocks]
    return pl.pallas_call(
        kernel,
        out_shape=outs,
        in_specs=[WHOLE] * len(ins),
        out_specs=[WHOLE] * len(outs),
        scratch_shapes=[pltpu.VMEM((2, keys, QUERY_TILE), jnp.float32)]
        + [narrow((keys, queries))] * (1 if apart else 2)
        + [
            pltpu.VMEM((keys // KEY_TILE, KEY_TILE // BLOCK, queries), jnp.float32),
            narrow((HEAD_DIM, keys)),
            narrow((HEAD_DIM + 16, keys)),
            narrow((HEAD_DIM, queries)),
            narrow((queries, HEAD_DIM)),
            pltpu.VMEM((1, queries), jnp.float32),
        ],
        compiler_params=pltpu.CompilerParams(vmem_limit_bytes=(60 if apart else 24) << 20),
    )(*ins)


def body(crews, team, queries, keys, values, grad_out, random_blocks, global_blocks):
    trade = functools.partial(
        lax.all_to_all, axis_name="lane", split_axis=0, concat_axis=0, tiled=True
    )
    tables = [random_blocks.transpose(2, 1, 0), global_blocks[None, :]]
    sent, *tables = pack([queries, grad_out, keys, values], tables)
    got = trade(sent)
    wide = []
    if crews > 1:
        wide = [lax.all_gather(got[:, a : a + 1], "crew", axis=0, tiled=True) for a in (2, 3)]
    back, *sums = attend(got, wide, *tables)
    sums = [lax.psum_scatter(x, "crew", scatter_dimension=0, tiled=True) for x in sums]
    if crews > 1:
        back = jnp.concatenate([back] + [x.astype(back.dtype) for x in sums], axis=1)
    return tuple(unpack(trade(back)))


def solution(mesh):
    devices = mesh.devices.reshape(-1)

    def run(queries, keys, values, grad_out, random_blocks, global_blocks):
        team = queries.shape[1] // HEAD_DIM
        crews = devices.size // team
        grid = Mesh(devices.reshape(crews, team), ("crew", "lane"))
        split = P(("crew", "lane"), None)
        return jax.shard_map(
            functools.partial(body, crews, team),
            mesh=grid,
            in_specs=(split,) * 4 + (P(), P()),
            out_specs=(split,) * 4,
            check_vma=False,
        )(queries, keys, values, grad_out, random_blocks, global_blocks)

    return run
```

```python
import functools
import math

import jax
import jax.numpy as jnp
from jax import lax
from jax.experimental import pallas as pl
from jax.experimental.pallas import tpu as pltpu
from jax.sharding import Mesh
from jax.sharding import PartitionSpec as P

HEAD_DIM = 128
BLOCK = 64
SCALE = HEAD_DIM**-0.5
QUERY_TILE = 256
KEY_TILE = 512
FAR_LANES = 4

WHOLE = pl.BlockSpec(memory_space=pltpu.VMEM)
FAR = pl.BlockSpec(memory_space=pltpu.HBM)


def dot(a, b):
    return lax.dot_general(a, b, (((1,), (0,)), ((), ())), preferred_element_type=jnp.float32)


def dot_nt(a, b):
    return lax.dot_general(a, b, (((1,), (1,)), ((), ())), preferred_element_type=jnp.float32)


def each(count, step, start):
    if count <= 4:
        carry = start
        for i in range(count):
            carry = step(i, carry)
        return carry
    return lax.fori_loop(0, count, step, start)


def copies(pairs, sems):
    made = [pltpu.make_async_copy(a, b, sems.at[i]) for i, (a, b) in enumerate(pairs)]
    for copy in made:
        copy.start()
    return made


def wait_all(made):
    for copy in made:
        copy.wait()


def pack_kernel(random_ref, global_ref, *refs):
    *ins, out, random_out, global_out, held, sems = refs
    pairs = [(x, held.at[a]) for a, x in enumerate(ins)]
    pairs += [(random_ref, random_out), (global_ref, global_out)]
    arriving = copies(pairs, sems)
    for a in range(len(ins)):
        arriving[a].wait()
        for h in range(out.shape[0]):
            out[h, a] = held[a, :, h * HEAD_DIM : (h + 1) * HEAD_DIM]
    wait_all(arriving[len(ins) :])


def pack(arrays, tables):
    rows, width = arrays[0].shape
    kind = arrays[0].dtype
    shape = (width // HEAD_DIM, len(arrays), rows, HEAD_DIM)
    ins = [pltpu.with_memory_space_constraint(x, pltpu.HBM) for x in tables + arrays]
    return pl.pallas_call(
        pack_kernel,
        out_shape=[pltpu.VMEM(shape, kind)] + [pltpu.VMEM(x.shape, x.dtype) for x in tables],
        in_specs=[FAR] * len(ins),
        out_specs=[WHOLE] * (1 + len(tables)),
        scratch_shapes=[
            pltpu.VMEM((len(arrays), rows, width), kind),
            pltpu.SemaphoreType.DMA((len(ins),)),
        ],
        compiler_params=pltpu.CompilerParams(vmem_limit_bytes=8 << 20),
    )(*ins)


def unpack_kernel(packed, *refs):
    outs, (held, sems) = refs[:-2], refs[-2:]
    leaving = []
    for a, out in enumerate(outs):
        for h in range(packed.shape[0]):
            held[a, :, h * HEAD_DIM : (h + 1) * HEAD_DIM] = packed[h, a]
        leaving.append(pltpu.make_async_copy(held.at[a], out, sems.at[a]))
        leaving[-1].start()
    wait_all(leaving)


def unpack(packed):
    heads, arrays, rows, depth = packed.shape
    return pl.pallas_call(
        unpack_kernel,
        out_shape=[jax.ShapeDtypeStruct((rows, heads * depth), packed.dtype)] * arrays,
        in_specs=[WHOLE],
        out_specs=[FAR] * arrays,
        scratch_shapes=[
            pltpu.VMEM((arrays, rows, heads * depth), packed.dtype),
            pltpu.SemaphoreType.DMA((arrays,)),
        ],
        compiler_params=pltpu.CompilerParams(vmem_limit_bytes=8 << 20),
    )(packed)


def place(order, lane):
    far, near = order
    team = far * near
    inside = lane % team
    return lane - inside + inside % near * far + inside // near


def tile_of(at, start, size):
    ref, slot, order = at
    rows = ref.shape[2]
    first = start // rows
    pieces = [ref[place(order, first + i), slot] for i in range(size // rows)]
    return jnp.concatenate(pieces, axis=0)


def put(at, start, tile):
    ref, slot, order = at
    rows = ref.shape[2]
    first = start // rows
    tile = tile.astype(ref.dtype)
    for i in range(tile.shape[0] // rows):
        ref[place(order, first + i), slot] = tile[i * rows : (i + 1) * rows]


def span(i, size):
    return pl.ds(pl.multiple_of(i * size, size), size)


def flip(at, out, length):
    step = min(512, length)

    def one(i, _):
        tile = tile_of(at, i * step, step)
        out[:HEAD_DIM, span(i, step)] = tile.astype(jnp.float32).T.astype(out.dtype)
        return 0

    each(length // step, one, 0)


def list_bias(random_ref, global_ref, bias_ref):
    steps, group, queries = bias_ref.shape
    blocks, total = queries // BLOCK, steps * group
    first = lax.axis_index("crew") * blocks
    shape = (blocks, total)
    names = lax.broadcasted_iota(jnp.int32, shape, 1)
    own = first + lax.broadcasted_iota(jnp.int32, shape, 0)
    times = (jnp.abs(names - own) <= 1).astype(jnp.float32)
    for i in range(global_ref.shape[1]):
        times += (names == global_ref[:, i : i + 1]).astype(jnp.float32)
    heads = random_ref.shape[2]
    head = lax.axis_index("near") * lax.axis_size("far") + lax.axis_index("far")
    mine = lax.broadcasted_iota(jnp.int32, (blocks, heads), 1) == head
    for i in range(random_ref.shape[0]):
        picks = jnp.where(mine, random_ref[i, pl.ds(first, blocks), :], 0)
        times += (names == jnp.sum(picks, axis=1, keepdims=True)).astype(jnp.float32)
    place = lax.broadcasted_iota(jnp.int32, (blocks, queries), 1) // BLOCK
    place = (place == lax.broadcasted_iota(jnp.int32, (blocks, queries), 0)).astype(jnp.bfloat16)
    wide = lax.dot_general(
        times.astype(jnp.bfloat16), place, (((0,), (0,)), ((), ())), preferred_element_type=jnp.float32
    )
    bias = jnp.where(wide > 0.0, jnp.log2(jnp.maximum(wide, 1.0)), -jnp.inf)
    bias_ref[...] = bias.reshape(steps, group, queries)


def attend_kernel(
    q_at, g_at, k_at, v_at, random_ref, global_ref, out_at, dq_at, dk_at, dv_at,
    score_ref, w_ref, ds_ref, bias_ref, kt_ref, vt_ref, gt_ref, gs_ref, delta_ref, sum_ref,
):
    keys, queries = w_ref.shape
    steps = keys // KEY_TILE
    turns = queries // QUERY_TILE
    factor = SCALE * math.log2(math.e)
    list_bias(random_ref, global_ref, bias_ref)
    flip(v_at, vt_ref, keys)
    vt_ref[HEAD_DIM:, :] = jnp.ones_like(vt_ref[HEAD_DIM:, :])

    def through(left_ref, right_ref, here):
        def add(c, total):
            at = span(c, KEY_TILE)
            return total + dot(left_ref[:, at], right_ref[at, here])

        if steps <= 4:
            return dot(left_ref[...], right_ref[:, here])
        return each(steps, add, jnp.zeros((left_ref.shape[0], QUERY_TILE), jnp.float32))

    def blocks_of(x):
        return x.reshape(KEY_TILE // BLOCK, BLOCK, QUERY_TILE)

    def score(t):
        here = span(t, QUERY_TILE)
        held = score_ref.at[t % score_ref.shape[0]]
        q = tile_of(q_at, t * QUERY_TILE, QUERY_TILE)

        def one(c, top):
            raw = dot_nt(tile_of(k_at, c * KEY_TILE, KEY_TILE), q)
            held[span(c, KEY_TILE), :] = raw
            listed = jnp.where(bias_ref[c, :, here] > -jnp.inf, 0.0, -jnp.inf)
            best = jnp.max(blocks_of(raw), axis=1) + listed
            return jnp.maximum(top, jnp.max(best, axis=0, keepdims=True))

        return each(steps, one, jnp.full((1, QUERY_TILE), -jnp.inf, jnp.float32)) * factor

    def weigh(t, top):
        here = span(t, QUERY_TILE)
        held = score_ref.at[t % score_ref.shape[0]]

        def one(c, _):
            at = span(c, KEY_TILE)
            shift = bias_ref[c, :, here] - top
            e = jnp.exp2(blocks_of(held[at, :]) * factor + shift[:, None, :])
            w_ref[at, here] = e.reshape(KEY_TILE, QUERY_TILE).astype(w_ref.dtype)
            return 0

        each(steps, one, 0)

    def mix(t):
        here = span(t, QUERY_TILE)
        mixed = through(vt_ref, w_ref, here)
        inverse = 1.0 / mixed[HEAD_DIM : HEAD_DIM + 1]
        out = (mixed[:HEAD_DIM] * inverse).astype(jnp.bfloat16).astype(jnp.float32)
        put(out_at, t * QUERY_TILE, out.T)
        g = tile_of(g_at, t * QUERY_TILE, QUERY_TILE).astype(jnp.float32).T
        delta_ref[:, here] = jnp.sum(g * out, axis=0, keepdims=True) * inverse
        g = g * inverse
        gt_ref[:, here] = g.astype(gt_ref.dtype)
        gs_ref[here, :] = g.T.astype(gs_ref.dtype)

    def back(t):
        here = span(t, QUERY_TILE)

        def one(c, _):
            at = span(c, KEY_TILE)
            gap = dot(tile_of(v_at, c * KEY_TILE, KEY_TILE), gt_ref[:, here]) - delta_ref[:, here]
            ds_ref[at, here] = (w_ref[at, here].astype(jnp.float32) * gap).astype(ds_ref.dtype)
            return 0

        each(steps, one, 0)
        put(dq_at, t * QUERY_TILE, (through(kt_ref, ds_ref, here) * SCALE).T)

    def collect(left_ref, right, out_at, slot, scale, first, last):
        here = pl.ds(first * QUERY_TILE, (last - first) * QUERY_TILE)

        def one(c, _):
            at = span(c, KEY_TILE)
            total = dot(left_ref[at, here], right)
            if first > 0:
                total += sum_ref[slot, at, :] if sum_ref is not None else tile_of(out_at, c * KEY_TILE, KEY_TILE)
            if last < turns and sum_ref is not None:
                sum_ref[slot, at, :] = total
            else:
                put(out_at, c * KEY_TILE, total * scale if last == turns else total)
            return 0

        each(steps, one, 0)

    def collect_values(first, last):
        here = pl.ds(first * QUERY_TILE, (last - first) * QUERY_TILE)
        collect(w_ref, gs_ref[here, :], dv_at, 0, 1.0, first, last)

    def collect_keys(first, last):
        q = tile_of(q_at, first * QUERY_TILE, (last - first) * QUERY_TILE)
        collect(ds_ref, q, dk_at, 1, SCALE, first, last)

    flip(k_at, kt_ref, keys)
    if sum_ref is None:
        for t in range(turns):
            weigh(t, score(t))
            mix(t)
            collect_values(t, t + 1)
            back(t)
        collect_keys(0, turns)
        return
    half = turns // 2
    tops = [score(0)]
    for t in range(turns + 1):
        if t + 1 < turns:
            tops.append(score(t + 1))
        if t < turns:
            weigh(t, tops[t])
            mix(t)
        if t > 0:
            back(t - 1)
        if t == half:
            collect_values(0, half)
            collect_keys(0, half)
    collect_values(half, turns)
    collect_keys(half, turns)


def attend(rows, wide, random_blocks, global_blocks, order):
    team, _, height, _ = rows.shape
    queries = team * height
    apart = len(wide) > 0
    keys = wide[0].shape[0] * height if apart else queries
    outs = [jax.ShapeDtypeStruct((team, 2 if apart else 4, height, HEAD_DIM), rows.dtype)]
    if apart:
        outs += [jax.ShapeDtypeStruct(x.shape, jnp.float32) for x in wide]

    def kernel(*refs):
        rows_ref, *refs = refs
        q_at, g_at, k_at, v_at = ((rows_ref, a, order) for a in range(4))
        if apart:
            k_at, v_at, *refs = [(refs[0], 0, order), (refs[1], 0, order)] + refs[2:]
        random_ref, global_ref, out_ref, *refs = refs
        out_at, dq_at, dk_at, dv_at = ((out_ref, a, order) for a in range(4))
        if apart:
            dk_at, dv_at, *refs = [(refs[0], 0, order), (refs[1], 0, order)] + refs[2:]
        score_ref, w_ref, *refs = refs
        ds_ref, *refs = [w_ref] + refs if apart else refs
        attend_kernel(
            q_at, g_at, k_at, v_at, random_ref, global_ref, out_at, dq_at, dk_at, dv_at,
            score_ref, w_ref, ds_ref, *refs[:6], *(refs[6:] or [None]),
        )

    narrow = functools.partial(pltpu.VMEM, dtype=rows.dtype)
    ins = [rows, *wide, random_blocks, global_blocks]
    return pl.pallas_call(
        kernel,
        out_shape=outs,
        in_specs=[WHOLE] * len(ins),
        out_specs=[WHOLE] * len(outs),
        scratch_shapes=[pltpu.VMEM((1 if apart else 2, keys, QUERY_TILE), jnp.float32)]
        + [narrow((keys, queries))] * (1 if apart else 2)
        + [
            pltpu.VMEM((keys // KEY_TILE, KEY_TILE // BLOCK, queries), jnp.float32),
            narrow((HEAD_DIM, keys)),
            narrow((HEAD_DIM + 16, keys)),
            narrow((HEAD_DIM, queries)),
            narrow((queries, HEAD_DIM)),
            pltpu.VMEM((1, queries), jnp.float32),
        ]
        + [pltpu.VMEM((2, keys, HEAD_DIM), jnp.float32)] * (not apart),
        compiler_params=pltpu.CompilerParams(vmem_limit_bytes=(60 if apart else 24) << 20),
    )(*ins)


def body(crews, order, queries, keys, values, grad_out, random_blocks, global_blocks):
    trade = functools.partial(
        lax.all_to_all, axis_name=("near", "far"), split_axis=0, concat_axis=0, tiled=True
    )
    tables = [random_blocks.transpose(2, 1, 0), global_blocks[None, :]]
    sent, *tables = pack([queries, grad_out, keys, values], tables)
    got = trade(sent)
    wide = []
    if crews > 1:
        wide = [lax.all_gather(got[:, a : a + 1], "crew", axis=0, tiled=True) for a in (2, 3)]
    back, *sums = attend(got, wide, *tables, order)
    sums = [lax.psum_scatter(x, "crew", scatter_dimension=0, tiled=True) for x in sums]
    if crews > 1:
        back = jnp.concatenate([back] + [x.astype(back.dtype) for x in sums], axis=1)
    return tuple(unpack(trade(back)))


def solution(mesh):
    devices = mesh.devices.reshape(-1)

    def run(queries, keys, values, grad_out, random_blocks, global_blocks):
        team = queries.shape[1] // HEAD_DIM
        crews = devices.size // team
        order = (FAR_LANES, team // FAR_LANES)
        grid = Mesh(devices.reshape(crews, *order), ("crew", "far", "near"))
        split = P(("crew", "far", "near"), None)
        return jax.shard_map(
            functools.partial(body, crews, order),
            mesh=grid,
            in_specs=(split,) * 4 + (P(), P()),
            out_specs=(split,) * 4,
            check_vma=False,
        )(queries, keys, values, grad_out, random_blocks, global_blocks)

    return run
```

```python
import functools
import math

import jax
import jax.numpy as jnp
from jax import lax
from jax.experimental import pallas as pl
from jax.experimental.pallas import tpu as pltpu
from jax.sharding import Mesh
from jax.sharding import PartitionSpec as P

HEAD_DIM = 128
BLOCK = 64
SCALE = HEAD_DIM**-0.5
QUERY_TILE = 256
KEY_TILE = 512
FAR_LANES = 4

WHOLE = pl.BlockSpec(memory_space=pltpu.VMEM)
FAR = pl.BlockSpec(memory_space=pltpu.HBM)


def dot(a, b):
    return lax.dot_general(a, b, (((1,), (0,)), ((), ())), preferred_element_type=jnp.float32)


def dot_nt(a, b):
    return lax.dot_general(a, b, (((1,), (1,)), ((), ())), preferred_element_type=jnp.float32)


def each(count, step, start):
    if count <= 4:
        carry = start
        for i in range(count):
            carry = step(i, carry)
        return carry
    return lax.fori_loop(0, count, step, start)


def copies(pairs, sems):
    made = [pltpu.make_async_copy(a, b, sems.at[i]) for i, (a, b) in enumerate(pairs)]
    for copy in made:
        copy.start()
    return made


def wait_all(made):
    for copy in made:
        copy.wait()


def pack_kernel(random_ref, global_ref, *refs):
    *ins, out, random_out, global_out, held, sems = refs
    pairs = [(x, held.at[a]) for a, x in enumerate(ins)]
    pairs += [(random_ref, random_out), (global_ref, global_out)]
    arriving = copies(pairs, sems)
    for a in range(len(ins)):
        arriving[a].wait()
        for h in range(out.shape[0]):
            out[h, a] = held[a, :, h * HEAD_DIM : (h + 1) * HEAD_DIM]
    wait_all(arriving[len(ins) :])


def pack(arrays, tables):
    rows, width = arrays[0].shape
    kind = arrays[0].dtype
    shape = (width // HEAD_DIM, len(arrays), rows, HEAD_DIM)
    ins = [pltpu.with_memory_space_constraint(x, pltpu.HBM) for x in tables + arrays]
    return pl.pallas_call(
        pack_kernel,
        out_shape=[pltpu.VMEM(shape, kind)] + [pltpu.VMEM(x.shape, x.dtype) for x in tables],
        in_specs=[FAR] * len(ins),
        out_specs=[WHOLE] * (1 + len(tables)),
        scratch_shapes=[
            pltpu.VMEM((len(arrays), rows, width), kind),
            pltpu.SemaphoreType.DMA((len(ins),)),
        ],
        compiler_params=pltpu.CompilerParams(vmem_limit_bytes=8 << 20),
    )(*ins)


def unpack_kernel(packed, *refs):
    outs, (held, sems) = refs[:-2], refs[-2:]
    leaving = []
    for a, out in enumerate(outs):
        for h in range(packed.shape[0]):
            held[a, :, h * HEAD_DIM : (h + 1) * HEAD_DIM] = packed[h, a]
        leaving.append(pltpu.make_async_copy(held.at[a], out, sems.at[a]))
        leaving[-1].start()
    wait_all(leaving)


def unpack(packed):
    heads, arrays, rows, depth = packed.shape
    return pl.pallas_call(
        unpack_kernel,
        out_shape=[jax.ShapeDtypeStruct((rows, heads * depth), packed.dtype)] * arrays,
        in_specs=[WHOLE],
        out_specs=[FAR] * arrays,
        scratch_shapes=[
            pltpu.VMEM((arrays, rows, heads * depth), packed.dtype),
            pltpu.SemaphoreType.DMA((arrays,)),
        ],
        compiler_params=pltpu.CompilerParams(vmem_limit_bytes=8 << 20),
    )(packed)


def place(order, lane):
    far, near = order
    team = far * near
    inside = lane % team
    return lane - inside + inside % near * far + inside // near


def tile_of(at, start, size):
    ref, slot, order = at
    rows = ref.shape[2]
    first = start // rows
    pieces = [ref[place(order, first + i), slot] for i in range(size // rows)]
    return jnp.concatenate(pieces, axis=0)


def put(at, start, tile):
    ref, slot, order = at
    rows = ref.shape[2]
    first = start // rows
    tile = tile.astype(ref.dtype)
    for i in range(tile.shape[0] // rows):
        ref[place(order, first + i), slot] = tile[i * rows : (i + 1) * rows]


def span(i, size):
    return pl.ds(pl.multiple_of(i * size, size), size)


def turned(x):
    size = (x.shape[1], x.shape[1])
    same = lax.broadcasted_iota(jnp.int32, size, 0) == lax.broadcasted_iota(jnp.int32, size, 1)
    return dot_nt(same.astype(x.dtype), x)


def flip(at, out, length):
    step = min(512, length)

    def one(i, _):
        tile = tile_of(at, i * step, step)
        out[:HEAD_DIM, span(i, step)] = turned(tile).astype(out.dtype)
        return 0

    each(length // step, one, 0)


def list_bias(random_ref, global_ref, bias_ref):
    steps, group, queries = bias_ref.shape
    blocks, total = queries // BLOCK, steps * group
    first = lax.axis_index("crew") * blocks
    shape = (blocks, total)
    names = lax.broadcasted_iota(jnp.int32, shape, 1)
    own = first + lax.broadcasted_iota(jnp.int32, shape, 0)
    times = (jnp.abs(names - own) <= 1).astype(jnp.float32)
    for i in range(global_ref.shape[1]):
        times += (names == global_ref[:, i : i + 1]).astype(jnp.float32)
    heads = random_ref.shape[2]
    head = lax.axis_index("near") * lax.axis_size("far") + lax.axis_index("far")
    mine = lax.broadcasted_iota(jnp.int32, (blocks, heads), 1) == head
    for i in range(random_ref.shape[0]):
        picks = jnp.where(mine, random_ref[i, pl.ds(first, blocks), :], 0)
        times += (names == jnp.sum(picks, axis=1, keepdims=True)).astype(jnp.float32)
    place = lax.broadcasted_iota(jnp.int32, (blocks, queries), 1) // BLOCK
    place = (place == lax.broadcasted_iota(jnp.int32, (blocks, queries), 0)).astype(jnp.bfloat16)
    wide = lax.dot_general(
        times.astype(jnp.bfloat16), place, (((0,), (0,)), ((), ())), preferred_element_type=jnp.float32
    )
    bias = jnp.where(wide > 0.0, jnp.log2(jnp.maximum(wide, 1.0)), -jnp.inf)
    bias_ref[...] = bias.reshape(steps, group, queries)


def attend_kernel(
    q_at, g_at, k_at, v_at, random_ref, global_ref, out_at, dq_at, dk_at, dv_at,
    score_ref, w_ref, ds_ref, bias_ref, kt_ref, vt_ref, gt_ref, gs_ref, delta_ref,
):
    keys, queries = w_ref.shape
    steps = keys // KEY_TILE
    turns = queries // QUERY_TILE
    factor = SCALE * math.log2(math.e)
    list_bias(random_ref, global_ref, bias_ref)
    flip(v_at, vt_ref, keys)
    vt_ref[HEAD_DIM:, :] = jnp.ones_like(vt_ref[HEAD_DIM:, :])

    def through(left_ref, right_ref, here):
        def add(c, total):
            at = span(c, KEY_TILE)
            return total + dot(left_ref[:, at], right_ref[at, here])

        if steps <= 4:
            return dot(left_ref[...], right_ref[:, here])
        return each(steps, add, jnp.zeros((left_ref.shape[0], QUERY_TILE), jnp.float32))

    def blocks_of(x):
        return x.reshape(KEY_TILE // BLOCK, BLOCK, QUERY_TILE)

    def score(t):
        here = span(t, QUERY_TILE)
        held = score_ref.at[t % 2]
        q = tile_of(q_at, t * QUERY_TILE, QUERY_TILE)

        def one(c, top):
            raw = dot_nt(tile_of(k_at, c * KEY_TILE, KEY_TILE), q)
            held[span(c, KEY_TILE), :] = raw
            listed = jnp.where(bias_ref[c, :, here] > -jnp.inf, 0.0, -jnp.inf)
            best = jnp.max(blocks_of(raw), axis=1) + listed
            return jnp.maximum(top, jnp.max(best, axis=0, keepdims=True))

        return each(steps, one, jnp.full((1, QUERY_TILE), -jnp.inf, jnp.float32)) * factor

    def weigh(t, top):
        here = span(t, QUERY_TILE)
        held = score_ref.at[t % 2]

        def one(c, _):
            at = span(c, KEY_TILE)
            shift = bias_ref[c, :, here] - top
            e = jnp.exp2(blocks_of(held[at, :]) * factor + shift[:, None, :])
            w_ref[at, here] = e.reshape(KEY_TILE, QUERY_TILE).astype(w_ref.dtype)
            return 0

        each(steps, one, 0)

    def mix(t):
        here = span(t, QUERY_TILE)
        mixed = through(vt_ref, w_ref, here)
        inverse = 1.0 / mixed[HEAD_DIM : HEAD_DIM + 1]
        out = (mixed[:HEAD_DIM] * inverse).astype(jnp.bfloat16)
        put(out_at, t * QUERY_TILE, turned(out))
        out = out.astype(jnp.float32)
        g = turned(tile_of(g_at, t * QUERY_TILE, QUERY_TILE))
        delta_ref[:, here] = jnp.sum(g * out, axis=0, keepdims=True) * inverse
        g = (g * inverse).astype(gt_ref.dtype)
        gt_ref[:, here] = g
        gs_ref[here, :] = turned(g).astype(gs_ref.dtype)

    tops = [score(0)]
    for t in range(turns):
        if t + 1 < turns:
            tops.append(score(t + 1))
        weigh(t, tops[t])
        mix(t)

    def backward(c, _):
        at = span(c, KEY_TILE)
        put(dv_at, c * KEY_TILE, dot(w_ref[at, :], gs_ref[...]))
        v = tile_of(v_at, c * KEY_TILE, KEY_TILE)
        for t in range(turns):
            here = span(t, QUERY_TILE)
            gap = dot(v, gt_ref[:, here]) - delta_ref[:, here]
            ds_ref[at, here] = (w_ref[at, here].astype(jnp.float32) * gap).astype(ds_ref.dtype)
        q = tile_of(q_at, 0, queries)
        put(dk_at, c * KEY_TILE, dot(ds_ref[at, :], q) * SCALE)
        return 0

    each(steps, backward, 0)
    flip(k_at, kt_ref, keys)
    for t in range(turns):
        dq = through(kt_ref, ds_ref, span(t, QUERY_TILE)) * SCALE
        put(dq_at, t * QUERY_TILE, turned(dq.astype(jnp.bfloat16)))


def attend(rows, wide, random_blocks, global_blocks, order):
    team, _, height, _ = rows.shape
    queries = team * height
    apart = len(wide) > 0
    keys = wide[0].shape[0] * height if apart else queries
    outs = [jax.ShapeDtypeStruct((team, 2 if apart else 4, height, HEAD_DIM), rows.dtype)]
    if apart:
        outs += [jax.ShapeDtypeStruct(x.shape, jnp.float32) for x in wide]

    def kernel(*refs):
        rows_ref, *refs = refs
        q_at, g_at, k_at, v_at = ((rows_ref, a, order) for a in range(4))
        if apart:
            k_at, v_at, *refs = [(refs[0], 0, order), (refs[1], 0, order)] + refs[2:]
        random_ref, global_ref, out_ref, *refs = refs
        out_at, dq_at, dk_at, dv_at = ((out_ref, a, order) for a in range(4))
        if apart:
            dk_at, dv_at, *refs = [(refs[0], 0, order), (refs[1], 0, order)] + refs[2:]
        score_ref, w_ref, *refs = refs
        ds_ref, *refs = [w_ref] + refs if apart else refs
        attend_kernel(
            q_at, g_at, k_at, v_at, random_ref, global_ref, out_at, dq_at, dk_at, dv_at,
            score_ref, w_ref, ds_ref, *refs,
        )

    narrow = functools.partial(pltpu.VMEM, dtype=rows.dtype)
    ins = [rows, *wide, random_blocks, global_blocks]
    return pl.pallas_call(
        kernel,
        out_shape=outs,
        in_specs=[WHOLE] * len(ins),
        out_specs=[WHOLE] * len(outs),
        scratch_shapes=[pltpu.VMEM((2, keys, QUERY_TILE), jnp.float32)]
        + [narrow((keys, queries))] * (1 if apart else 2)
        + [
            pltpu.VMEM((keys // KEY_TILE, KEY_TILE // BLOCK, queries), jnp.float32),
            narrow((HEAD_DIM, keys)),
            narrow((HEAD_DIM + 16, keys)),
            narrow((HEAD_DIM, queries)),
            narrow((queries, HEAD_DIM)),
            pltpu.VMEM((1, queries), jnp.float32),
        ],
        compiler_params=pltpu.CompilerParams(vmem_limit_bytes=(60 if apart else 24) << 20),
    )(*ins)


def body(crews, order, queries, keys, values, grad_out, random_blocks, global_blocks):
    trade = functools.partial(
        lax.all_to_all, axis_name=("near", "far"), split_axis=0, concat_axis=0, tiled=True
    )
    tables = [random_blocks.transpose(2, 1, 0), global_blocks[None, :]]
    sent, *tables = pack([queries, grad_out, keys, values], tables)
    got = trade(sent)
    wide = []
    if crews > 1:
        wide = [lax.all_gather(got[:, a : a + 1], "crew", axis=0, tiled=True) for a in (2, 3)]
    back, *sums = attend(got, wide, *tables, order)
    sums = [lax.psum_scatter(x, "crew", scatter_dimension=0, tiled=True) for x in sums]
    if crews > 1:
        back = jnp.concatenate([back] + [x.astype(back.dtype) for x in sums], axis=1)
    return tuple(unpack(trade(back)))


def solution(mesh):
    devices = mesh.devices.reshape(-1)

    def run(queries, keys, values, grad_out, random_blocks, global_blocks):
        team = queries.shape[1] // HEAD_DIM
        crews = devices.size // team
        order = (FAR_LANES, team // FAR_LANES)
        grid = Mesh(devices.reshape(crews, *order), ("crew", "far", "near"))
        split = P(("crew", "far", "near"), None)
        return jax.shard_map(
            functools.partial(body, crews, order),
            mesh=grid,
            in_specs=(split,) * 4 + (P(), P()),
            out_specs=(split,) * 4,
            check_vma=False,
        )(queries, keys, values, grad_out, random_blocks, global_blocks)

    return run
```

```python
import functools
import math

import jax
import jax.numpy as jnp
from jax import lax
from jax.experimental import pallas as pl
from jax.experimental.pallas import tpu as pltpu
from jax.sharding import Mesh
from jax.sharding import PartitionSpec as P

HEAD_DIM = 128
BLOCK = 64
SCALE = HEAD_DIM**-0.5
QUERY_TILE = 256
KEY_TILE = 512
FAR_LANES = 4

WHOLE = pl.BlockSpec(memory_space=pltpu.VMEM)
FAR = pl.BlockSpec(memory_space=pltpu.HBM)


def dot(a, b):
    return lax.dot_general(a, b, (((1,), (0,)), ((), ())), preferred_element_type=jnp.float32)


def each(count, step, start):
    if count <= 4:
        carry = start
        for i in range(count):
            carry = step(i, carry)
        return carry
    return lax.fori_loop(0, count, step, start)


def copies(pairs, sems):
    made = [pltpu.make_async_copy(a, b, sems.at[i]) for i, (a, b) in enumerate(pairs)]
    for copy in made:
        copy.start()
    return made


def wait_all(made):
    for copy in made:
        copy.wait()


def pack_kernel(random_ref, global_ref, *refs):
    *ins, out, random_out, global_out, held, sems = refs
    pairs = [(x, held.at[a]) for a, x in enumerate(ins)]
    pairs += [(random_ref, random_out), (global_ref, global_out)]
    arriving = copies(pairs, sems)
    for a in range(len(ins)):
        arriving[a].wait()
        for h in range(out.shape[0]):
            out[h, a] = held[a, :, h * HEAD_DIM : (h + 1) * HEAD_DIM]
    wait_all(arriving[len(ins) :])


def pack(arrays, tables):
    rows, width = arrays[0].shape
    kind = arrays[0].dtype
    shape = (width // HEAD_DIM, len(arrays), rows, HEAD_DIM)
    ins = [pltpu.with_memory_space_constraint(x, pltpu.HBM) for x in tables + arrays]
    return pl.pallas_call(
        pack_kernel,
        out_shape=[pltpu.VMEM(shape, kind)] + [pltpu.VMEM(x.shape, x.dtype) for x in tables],
        in_specs=[FAR] * len(ins),
        out_specs=[WHOLE] * (1 + len(tables)),
        scratch_shapes=[
            pltpu.VMEM((len(arrays), rows, width), kind),
            pltpu.SemaphoreType.DMA((len(ins),)),
        ],
        compiler_params=pltpu.CompilerParams(vmem_limit_bytes=8 << 20),
    )(*ins)


def unpack_kernel(packed, *refs):
    outs, (held, sems) = refs[:-2], refs[-2:]
    leaving = []
    for a, out in enumerate(outs):
        for h in range(packed.shape[0]):
            held[a, :, h * HEAD_DIM : (h + 1) * HEAD_DIM] = packed[h, a]
        leaving.append(pltpu.make_async_copy(held.at[a], out, sems.at[a]))
        leaving[-1].start()
    wait_all(leaving)


def unpack(packed):
    heads, arrays, rows, depth = packed.shape
    return pl.pallas_call(
        unpack_kernel,
        out_shape=[jax.ShapeDtypeStruct((rows, heads * depth), packed.dtype)] * arrays,
        in_specs=[WHOLE],
        out_specs=[FAR] * arrays,
        scratch_shapes=[
            pltpu.VMEM((arrays, rows, heads * depth), packed.dtype),
            pltpu.SemaphoreType.DMA((arrays,)),
        ],
        compiler_params=pltpu.CompilerParams(vmem_limit_bytes=8 << 20),
    )(packed)


def place(order, lane):
    far, near = order
    team = far * near
    inside = lane % team
    return lane - inside + inside % near * far + inside // near


def tile_of(at, start, size):
    ref, slot, order = at
    rows = ref.shape[2]
    first = start // rows
    pieces = [ref[place(order, first + i), slot] for i in range(size // rows)]
    return jnp.concatenate(pieces, axis=0)


def put(at, start, tile):
    ref, slot, order = at
    rows = ref.shape[2]
    first = start // rows
    tile = tile.astype(ref.dtype)
    for i in range(tile.shape[0] // rows):
        ref[place(order, first + i), slot] = tile[i * rows : (i + 1) * rows]


def span(i, size):
    return pl.ds(pl.multiple_of(i * size, size), size)


def flip(at, out, length):
    step = min(512, length)

    def one(i, _):
        tile = tile_of(at, i * step, step)
        out[:HEAD_DIM, span(i, step)] = tile.astype(jnp.float32).T.astype(out.dtype)
        return 0

    each(length // step, one, 0)


def list_bias(random_ref, global_ref, bias_ref):
    steps, group, queries = bias_ref.shape
    blocks, total = queries // BLOCK, steps * group
    first = lax.axis_index("crew") * blocks
    shape = (blocks, total)
    names = lax.broadcasted_iota(jnp.int32, shape, 1)
    own = first + lax.broadcasted_iota(jnp.int32, shape, 0)
    times = (jnp.abs(names - own) <= 1).astype(jnp.float32)
    for i in range(global_ref.shape[1]):
        times += (names == global_ref[:, i : i + 1]).astype(jnp.float32)
    heads = random_ref.shape[2]
    head = lax.axis_index("near") * lax.axis_size("far") + lax.axis_index("far")
    mine = lax.broadcasted_iota(jnp.int32, (blocks, heads), 1) == head
    for i in range(random_ref.shape[0]):
        picks = jnp.where(mine, random_ref[i, pl.ds(first, blocks), :], 0)
        times += (names == jnp.sum(picks, axis=1, keepdims=True)).astype(jnp.float32)
    place = lax.broadcasted_iota(jnp.int32, (blocks, queries), 1) // BLOCK
    place = (place == lax.broadcasted_iota(jnp.int32, (blocks, queries), 0)).astype(jnp.bfloat16)
    wide = lax.dot_general(
        times.astype(jnp.bfloat16), place, (((0,), (0,)), ((), ())), preferred_element_type=jnp.float32
    )
    bias = jnp.where(wide > 0.0, jnp.log2(jnp.maximum(wide, 1.0)), -jnp.inf)
    bias_ref[...] = bias.reshape(steps, group, queries)


def attend_kernel(
    q_at, g_at, k_at, v_at, random_ref, global_ref, out_at, dq_at, dk_at, dv_at,
    score_ref, w_ref, ds_ref, bias_ref, kt_ref, vt_ref, gt_ref, gs_ref, delta_ref,
):
    keys, queries = w_ref.shape
    steps = keys // KEY_TILE
    turns = queries // QUERY_TILE
    factor = SCALE * math.log2(math.e)
    list_bias(random_ref, global_ref, bias_ref)
    flip(v_at, vt_ref, keys)
    vt_ref[HEAD_DIM:, :] = jnp.ones_like(vt_ref[HEAD_DIM:, :])

    def through(left_ref, right_ref, here):
        def add(c, total):
            at = span(c, KEY_TILE)
            return total + dot(left_ref[:, at], right_ref[at, here])

        if steps <= 4:
            return dot(left_ref[...], right_ref[:, here])
        return each(steps, add, jnp.zeros((left_ref.shape[0], QUERY_TILE), jnp.float32))

    def blocks_of(x):
        return x.reshape(KEY_TILE // BLOCK, BLOCK, QUERY_TILE)

    def score(t):
        here = span(t, QUERY_TILE)
        held = score_ref.at[t % 2]
        q = tile_of(q_at, t * QUERY_TILE, QUERY_TILE).astype(jnp.float32).T.astype(jnp.bfloat16)

        def one(c, top):
            raw = dot(tile_of(k_at, c * KEY_TILE, KEY_TILE), q)
            held[span(c, KEY_TILE), :] = raw
            listed = jnp.where(bias_ref[c, :, here] > -jnp.inf, 0.0, -jnp.inf)
            best = jnp.max(blocks_of(raw), axis=1) + listed
            return jnp.maximum(top, jnp.max(best, axis=0, keepdims=True))

        return each(steps, one, jnp.full((1, QUERY_TILE), -jnp.inf, jnp.float32)) * factor

    def weigh(t, top):
        here = span(t, QUERY_TILE)
        held = score_ref.at[t % 2]

        def one(c, _):
            at = span(c, KEY_TILE)
            shift = bias_ref[c, :, here] - top
            e = jnp.exp2(blocks_of(held[at, :]) * factor + shift[:, None, :])
            w_ref[at, here] = e.reshape(KEY_TILE, QUERY_TILE).astype(w_ref.dtype)
            return 0

        each(steps, one, 0)

    def mix(t):
        here = span(t, QUERY_TILE)
        mixed = through(vt_ref, w_ref, here)
        inverse = 1.0 / mixed[HEAD_DIM : HEAD_DIM + 1]
        out = (mixed[:HEAD_DIM] * inverse).astype(jnp.bfloat16).astype(jnp.float32)
        put(out_at, t * QUERY_TILE, out.T)
        g = tile_of(g_at, t * QUERY_TILE, QUERY_TILE).astype(jnp.float32).T
        delta_ref[:, here] = jnp.sum(g * out, axis=0, keepdims=True) * inverse
        g = g * inverse
        gt_ref[:, here] = g.astype(gt_ref.dtype)
        gs_ref[here, :] = g.T.astype(gs_ref.dtype)

    tops = [score(0)]
    for t in range(turns):
        if t + 1 < turns:
            tops.append(score(t + 1))
        weigh(t, tops[t])
        mix(t)

    def backward(c, _):
        at = span(c, KEY_TILE)
        put(dv_at, c * KEY_TILE, dot(w_ref[at, :], gs_ref[...]))
        v = tile_of(v_at, c * KEY_TILE, KEY_TILE)
        for t in range(turns):
            here = span(t, QUERY_TILE)
            gap = dot(v, gt_ref[:, here]) - delta_ref[:, here]
            ds_ref[at, here] = (w_ref[at, here].astype(jnp.float32) * gap).astype(ds_ref.dtype)
        q = tile_of(q_at, 0, queries)
        put(dk_at, c * KEY_TILE, dot(ds_ref[at, :], q) * SCALE)
        return 0

    each(steps, backward, 0)
    flip(k_at, kt_ref, keys)
    for t in range(turns):
        put(dq_at, t * QUERY_TILE, (through(kt_ref, ds_ref, span(t, QUERY_TILE)) * SCALE).T)


def attend(rows, wide, random_blocks, global_blocks, order):
    team, _, height, _ = rows.shape
    queries = team * height
    apart = len(wide) > 0
    keys = wide[0].shape[0] * height if apart else queries
    outs = [jax.ShapeDtypeStruct((team, 2 if apart else 4, height, HEAD_DIM), rows.dtype)]
    if apart:
        outs += [jax.ShapeDtypeStruct(x.shape, jnp.float32) for x in wide]

    def kernel(*refs):
        rows_ref, *refs = refs
        q_at, g_at, k_at, v_at = ((rows_ref, a, order) for a in range(4))
        if apart:
            k_at, v_at, *refs = [(refs[0], 0, order), (refs[1], 0, order)] + refs[2:]
        random_ref, global_ref, out_ref, *refs = refs
        out_at, dq_at, dk_at, dv_at = ((out_ref, a, order) for a in range(4))
        if apart:
            dk_at, dv_at, *refs = [(refs[0], 0, order), (refs[1], 0, order)] + refs[2:]
        score_ref, w_ref, *refs = refs
        ds_ref, *refs = [w_ref] + refs if apart else refs
        attend_kernel(
            q_at, g_at, k_at, v_at, random_ref, global_ref, out_at, dq_at, dk_at, dv_at,
            score_ref, w_ref, ds_ref, *refs,
        )

    narrow = functools.partial(pltpu.VMEM, dtype=rows.dtype)
    ins = [rows, *wide, random_blocks, global_blocks]
    return pl.pallas_call(
        kernel,
        out_shape=outs,
        in_specs=[WHOLE] * len(ins),
        out_specs=[WHOLE] * len(outs),
        scratch_shapes=[pltpu.VMEM((2, keys, QUERY_TILE), jnp.float32)]
        + [narrow((keys, queries))] * (1 if apart else 2)
        + [
            pltpu.VMEM((keys // KEY_TILE, KEY_TILE // BLOCK, queries), jnp.float32),
            narrow((HEAD_DIM, keys)),
            narrow((HEAD_DIM + 16, keys)),
            narrow((HEAD_DIM, queries)),
            narrow((queries, HEAD_DIM)),
            pltpu.VMEM((1, queries), jnp.float32),
        ],
        compiler_params=pltpu.CompilerParams(vmem_limit_bytes=(60 if apart else 24) << 20),
    )(*ins)


def body(crews, order, queries, keys, values, grad_out, random_blocks, global_blocks):
    trade = functools.partial(
        lax.all_to_all, axis_name=("near", "far"), split_axis=0, concat_axis=0, tiled=True
    )
    tables = [random_blocks.transpose(2, 1, 0), global_blocks[None, :]]
    sent, *tables = pack([queries, grad_out, keys, values], tables)
    got = trade(sent)
    wide = []
    if crews > 1:
        wide = [lax.all_gather(got[:, a : a + 1], "crew", axis=0, tiled=True) for a in (2, 3)]
    back, *sums = attend(got, wide, *tables, order)
    sums = [lax.psum_scatter(x, "crew", scatter_dimension=0, tiled=True) for x in sums]
    if crews > 1:
        back = jnp.concatenate([back] + [x.astype(back.dtype) for x in sums], axis=1)
    return tuple(unpack(trade(back)))


def solution(mesh):
    devices = mesh.devices.reshape(-1)

    def run(queries, keys, values, grad_out, random_blocks, global_blocks):
        team = queries.shape[1] // HEAD_DIM
        crews = devices.size // team
        order = (FAR_LANES, team // FAR_LANES)
        grid = Mesh(devices.reshape(crews, *order), ("crew", "far", "near"))
        split = P(("crew", "far", "near"), None)
        return jax.shard_map(
            functools.partial(body, crews, order),
            mesh=grid,
            in_specs=(split,) * 4 + (P(), P()),
            out_specs=(split,) * 4,
            check_vma=False,
        )(queries, keys, values, grad_out, random_blocks, global_blocks)

    return run
```

```python
import functools
import math

import jax
import jax.numpy as jnp
from jax import lax
from jax.experimental import pallas as pl
from jax.experimental.pallas import tpu as pltpu
from jax.sharding import Mesh
from jax.sharding import PartitionSpec as P

HEAD_DIM = 128
BLOCK = 64
SCALE = HEAD_DIM**-0.5
QUERY_TILE = 256
KEY_TILE = 1024
FAR_LANES = 4

WHOLE = pl.BlockSpec(memory_space=pltpu.VMEM)
FAR = pl.BlockSpec(memory_space=pltpu.HBM)


def dot(a, b):
    return lax.dot_general(a, b, (((1,), (0,)), ((), ())), preferred_element_type=jnp.float32)


def each(count, step, start):
    if count <= 4:
        carry = start
        for i in range(count):
            carry = step(i, carry)
        return carry
    return lax.fori_loop(0, count, step, start)


def copies(pairs, sems):
    made = [pltpu.make_async_copy(a, b, sems.at[i]) for i, (a, b) in enumerate(pairs)]
    for copy in made:
        copy.start()
    return made


def wait_all(made):
    for copy in made:
        copy.wait()


def pack_kernel(random_ref, global_ref, *refs):
    *ins, out, random_out, global_out, held, sems = refs
    pairs = [(x, held.at[a]) for a, x in enumerate(ins)]
    pairs += [(random_ref, random_out), (global_ref, global_out)]
    arriving = copies(pairs, sems)
    for a in range(len(ins)):
        arriving[a].wait()
        for h in range(out.shape[0]):
            out[h, a] = held[a, :, h * HEAD_DIM : (h + 1) * HEAD_DIM]
    wait_all(arriving[len(ins) :])


def pack(arrays, tables):
    rows, width = arrays[0].shape
    kind = arrays[0].dtype
    shape = (width // HEAD_DIM, len(arrays), rows, HEAD_DIM)
    ins = [pltpu.with_memory_space_constraint(x, pltpu.HBM) for x in tables + arrays]
    return pl.pallas_call(
        pack_kernel,
        out_shape=[pltpu.VMEM(shape, kind)] + [pltpu.VMEM(x.shape, x.dtype) for x in tables],
        in_specs=[FAR] * len(ins),
        out_specs=[WHOLE] * (1 + len(tables)),
        scratch_shapes=[
            pltpu.VMEM((len(arrays), rows, width), kind),
            pltpu.SemaphoreType.DMA((len(ins),)),
        ],
        compiler_params=pltpu.CompilerParams(vmem_limit_bytes=8 << 20),
    )(*ins)


def unpack_kernel(packed, *refs):
    outs, (held, sems) = refs[:-2], refs[-2:]
    leaving = []
    for a, out in enumerate(outs):
        for h in range(packed.shape[0]):
            held[a, :, h * HEAD_DIM : (h + 1) * HEAD_DIM] = packed[h, a]
        leaving.append(pltpu.make_async_copy(held.at[a], out, sems.at[a]))
        leaving[-1].start()
    wait_all(leaving)


def unpack(packed):
    heads, arrays, rows, depth = packed.shape
    return pl.pallas_call(
        unpack_kernel,
        out_shape=[jax.ShapeDtypeStruct((rows, heads * depth), packed.dtype)] * arrays,
        in_specs=[WHOLE],
        out_specs=[FAR] * arrays,
        scratch_shapes=[
            pltpu.VMEM((arrays, rows, heads * depth), packed.dtype),
            pltpu.SemaphoreType.DMA((arrays,)),
        ],
        compiler_params=pltpu.CompilerParams(vmem_limit_bytes=8 << 20),
    )(packed)


def place(order, lane):
    far, near = order
    team = far * near
    inside = lane % team
    return lane - inside + inside % near * far + inside // near


def tile_of(at, start, size):
    ref, slot, order = at
    rows = ref.shape[2]
    first = start // rows
    pieces = [ref[place(order, first + i), slot] for i in range(size // rows)]
    return jnp.concatenate(pieces, axis=0)


def put(at, start, tile):
    ref, slot, order = at
    rows = ref.shape[2]
    first = start // rows
    tile = tile.astype(ref.dtype)
    for i in range(tile.shape[0] // rows):
        ref[place(order, first + i), slot] = tile[i * rows : (i + 1) * rows]


def span(i, size):
    return pl.ds(pl.multiple_of(i * size, size), size)


def flip(at, out, length):
    step = min(512, length)

    def one(i, _):
        tile = tile_of(at, i * step, step)
        out[:HEAD_DIM, span(i, step)] = tile.astype(jnp.float32).T.astype(out.dtype)
        return 0

    each(length // step, one, 0)


def list_bias(random_ref, global_ref, bias_ref):
    steps, group, queries = bias_ref.shape
    blocks, total = queries // BLOCK, steps * group
    first = lax.axis_index("crew") * blocks
    shape = (blocks, total)
    names = lax.broadcasted_iota(jnp.int32, shape, 1)
    own = first + lax.broadcasted_iota(jnp.int32, shape, 0)
    times = (jnp.abs(names - own) <= 1).astype(jnp.float32)
    for i in range(global_ref.shape[1]):
        times += (names == global_ref[:, i : i + 1]).astype(jnp.float32)
    heads = random_ref.shape[2]
    head = lax.axis_index("near") * lax.axis_size("far") + lax.axis_index("far")
    mine = lax.broadcasted_iota(jnp.int32, (blocks, heads), 1) == head
    for i in range(random_ref.shape[0]):
        picks = jnp.where(mine, random_ref[i, pl.ds(first, blocks), :], 0)
        times += (names == jnp.sum(picks, axis=1, keepdims=True)).astype(jnp.float32)
    place = lax.broadcasted_iota(jnp.int32, (blocks, queries), 1) // BLOCK
    place = (place == lax.broadcasted_iota(jnp.int32, (blocks, queries), 0)).astype(jnp.bfloat16)
    wide = lax.dot_general(
        times.astype(jnp.bfloat16), place, (((0,), (0,)), ((), ())), preferred_element_type=jnp.float32
    )
    bias = jnp.where(wide > 0.0, jnp.log2(jnp.maximum(wide, 1.0)), -jnp.inf)
    bias_ref[...] = bias.reshape(steps, group, queries)


def attend_kernel(
    q_at, g_at, k_at, v_at, random_ref, global_ref, out_at, dq_at, dk_at, dv_at,
    score_ref, w_ref, ds_ref, bias_ref, kt_ref, vt_ref, gt_ref, gs_ref, delta_ref,
):
    keys, queries = w_ref.shape
    steps = keys // KEY_TILE
    turns = queries // QUERY_TILE
    factor = SCALE * math.log2(math.e)
    list_bias(random_ref, global_ref, bias_ref)
    flip(v_at, vt_ref, keys)
    vt_ref[HEAD_DIM:, :] = jnp.ones_like(vt_ref[HEAD_DIM:, :])

    def through(left_ref, right_ref, here):
        def add(c, total):
            at = span(c, KEY_TILE)
            return total + dot(left_ref[:, at], right_ref[at, here])

        if steps <= 4:
            return dot(left_ref[...], right_ref[:, here])
        return each(steps, add, jnp.zeros((left_ref.shape[0], QUERY_TILE), jnp.float32))

    def blocks_of(x):
        return x.reshape(KEY_TILE // BLOCK, BLOCK, QUERY_TILE)

    def score(t):
        here = span(t, QUERY_TILE)
        held = score_ref.at[t % 2]
        q = tile_of(q_at, t * QUERY_TILE, QUERY_TILE).astype(jnp.float32).T.astype(jnp.bfloat16)

        def one(c, top):
            raw = dot(tile_of(k_at, c * KEY_TILE, KEY_TILE), q)
            held[span(c, KEY_TILE), :] = raw
            listed = jnp.where(bias_ref[c, :, here] > -jnp.inf, 0.0, -jnp.inf)
            best = jnp.max(blocks_of(raw), axis=1) + listed
            return jnp.maximum(top, jnp.max(best, axis=0, keepdims=True))

        return each(steps, one, jnp.full((1, QUERY_TILE), -jnp.inf, jnp.float32)) * factor

    def weigh(t, top):
        here = span(t, QUERY_TILE)
        held = score_ref.at[t % 2]

        def one(c, _):
            at = span(c, KEY_TILE)
            shift = bias_ref[c, :, here] - top
            e = jnp.exp2(blocks_of(held[at, :]) * factor + shift[:, None, :])
            w_ref[at, here] = e.reshape(KEY_TILE, QUERY_TILE).astype(w_ref.dtype)
            return 0

        each(steps, one, 0)

    def mix(t):
        here = span(t, QUERY_TILE)
        mixed = through(vt_ref, w_ref, here)
        inverse = 1.0 / mixed[HEAD_DIM : HEAD_DIM + 1]
        out = (mixed[:HEAD_DIM] * inverse).astype(jnp.bfloat16).astype(jnp.float32)
        put(out_at, t * QUERY_TILE, out.T)
        g = tile_of(g_at, t * QUERY_TILE, QUERY_TILE).astype(jnp.float32).T
        delta_ref[:, here] = jnp.sum(g * out, axis=0, keepdims=True) * inverse
        g = g * inverse
        gt_ref[:, here] = g.astype(gt_ref.dtype)
        gs_ref[here, :] = g.T.astype(gs_ref.dtype)

    tops = [score(0)]
    for t in range(turns):
        if t + 1 < turns:
            tops.append(score(t + 1))
        weigh(t, tops[t])
        mix(t)

    def backward(c, _):
        at = span(c, KEY_TILE)
        put(dv_at, c * KEY_TILE, dot(w_ref[at, :], gs_ref[...]))
        v = tile_of(v_at, c * KEY_TILE, KEY_TILE)
        for t in range(turns):
            here = span(t, QUERY_TILE)
            gap = dot(v, gt_ref[:, here]) - delta_ref[:, here]
            ds_ref[at, here] = (w_ref[at, here].astype(jnp.float32) * gap).astype(ds_ref.dtype)
        q = tile_of(q_at, 0, queries)
        put(dk_at, c * KEY_TILE, dot(ds_ref[at, :], q) * SCALE)
        return 0

    each(steps, backward, 0)
    flip(k_at, kt_ref, keys)
    for t in range(turns):
        put(dq_at, t * QUERY_TILE, (through(kt_ref, ds_ref, span(t, QUERY_TILE)) * SCALE).T)


def attend(rows, wide, random_blocks, global_blocks, order):
    team, _, height, _ = rows.shape
    queries = team * height
    apart = len(wide) > 0
    keys = wide[0].shape[0] * height if apart else queries
    outs = [jax.ShapeDtypeStruct((team, 2 if apart else 4, height, HEAD_DIM), rows.dtype)]
    if apart:
        outs += [jax.ShapeDtypeStruct(x.shape, jnp.float32) for x in wide]

    def kernel(*refs):
        rows_ref, *refs = refs
        q_at, g_at, k_at, v_at = ((rows_ref, a, order) for a in range(4))
        if apart:
            k_at, v_at, *refs = [(refs[0], 0, order), (refs[1], 0, order)] + refs[2:]
        random_ref, global_ref, out_ref, *refs = refs
        out_at, dq_at, dk_at, dv_at = ((out_ref, a, order) for a in range(4))
        if apart:
            dk_at, dv_at, *refs = [(refs[0], 0, order), (refs[1], 0, order)] + refs[2:]
        score_ref, w_ref, *refs = refs
        ds_ref, *refs = [w_ref] + refs if apart else refs
        attend_kernel(
            q_at, g_at, k_at, v_at, random_ref, global_ref, out_at, dq_at, dk_at, dv_at,
            score_ref, w_ref, ds_ref, *refs,
        )

    narrow = functools.partial(pltpu.VMEM, dtype=rows.dtype)
    ins = [rows, *wide, random_blocks, global_blocks]
    return pl.pallas_call(
        kernel,
        out_shape=outs,
        in_specs=[WHOLE] * len(ins),
        out_specs=[WHOLE] * len(outs),
        scratch_shapes=[pltpu.VMEM((2, keys, QUERY_TILE), jnp.float32)]
        + [narrow((keys, queries))] * (1 if apart else 2)
        + [
            pltpu.VMEM((keys // KEY_TILE, KEY_TILE // BLOCK, queries), jnp.float32),
            narrow((HEAD_DIM, keys)),
            narrow((HEAD_DIM + 16, keys)),
            narrow((HEAD_DIM, queries)),
            narrow((queries, HEAD_DIM)),
            pltpu.VMEM((1, queries), jnp.float32),
        ],
        compiler_params=pltpu.CompilerParams(vmem_limit_bytes=(60 if apart else 24) << 20),
    )(*ins)


def body(crews, order, queries, keys, values, grad_out, random_blocks, global_blocks):
    trade = functools.partial(
        lax.all_to_all, axis_name=("near", "far"), split_axis=0, concat_axis=0, tiled=True
    )
    tables = [random_blocks.transpose(2, 1, 0), global_blocks[None, :]]
    sent, *tables = pack([queries, grad_out, keys, values], tables)
    got = trade(sent)
    wide = []
    if crews > 1:
        wide = [lax.all_gather(got[:, a : a + 1], "crew", axis=0, tiled=True) for a in (2, 3)]
    back, *sums = attend(got, wide, *tables, order)
    sums = [lax.psum_scatter(x, "crew", scatter_dimension=0, tiled=True) for x in sums]
    if crews > 1:
        back = jnp.concatenate([back] + [x.astype(back.dtype) for x in sums], axis=1)
    return tuple(unpack(trade(back)))


def solution(mesh):
    devices = mesh.devices.reshape(-1)

    def run(queries, keys, values, grad_out, random_blocks, global_blocks):
        team = queries.shape[1] // HEAD_DIM
        crews = devices.size // team
        order = (FAR_LANES, team // FAR_LANES)
        grid = Mesh(devices.reshape(crews, *order), ("crew", "far", "near"))
        split = P(("crew", "far", "near"), None)
        return jax.shard_map(
            functools.partial(body, crews, order),
            mesh=grid,
            in_specs=(split,) * 4 + (P(), P()),
            out_specs=(split,) * 4,
            check_vma=False,
        )(queries, keys, values, grad_out, random_blocks, global_blocks)

    return run
```

```python
import functools
import math

import jax
import jax.numpy as jnp
from jax import lax
from jax.experimental import pallas as pl
from jax.experimental.pallas import tpu as pltpu
from jax.sharding import Mesh
from jax.sharding import PartitionSpec as P

HEAD_DIM = 128
BLOCK = 64
SCALE = HEAD_DIM**-0.5
QUERY_TILE = 256
KEY_TILE = 512
FAR_LANES = 4

WHOLE = pl.BlockSpec(memory_space=pltpu.VMEM)
FAR = pl.BlockSpec(memory_space=pltpu.HBM)


def dot(a, b):
    return lax.dot_general(a, b, (((1,), (0,)), ((), ())), preferred_element_type=jnp.float32)


def each(count, step, start):
    if count <= 4:
        carry = start
        for i in range(count):
            carry = step(i, carry)
        return carry
    return lax.fori_loop(0, count, step, start)


def copies(pairs, sems):
    made = [pltpu.make_async_copy(a, b, sems.at[i]) for i, (a, b) in enumerate(pairs)]
    for copy in made:
        copy.start()
    return made


def wait_all(made):
    for copy in made:
        copy.wait()


def pack_kernel(random_ref, global_ref, *refs):
    *ins, out, random_out, global_out, held, sems = refs
    pairs = [(x, held.at[a]) for a, x in enumerate(ins)]
    pairs += [(random_ref, random_out), (global_ref, global_out)]
    arriving = copies(pairs, sems)
    for a in range(len(ins)):
        arriving[a].wait()
        for h in range(out.shape[0]):
            out[h, a] = held[a, :, h * HEAD_DIM : (h + 1) * HEAD_DIM]
    wait_all(arriving[len(ins) :])


def pack(arrays, tables):
    rows, width = arrays[0].shape
    kind = arrays[0].dtype
    shape = (width // HEAD_DIM, len(arrays), rows, HEAD_DIM)
    ins = [pltpu.with_memory_space_constraint(x, pltpu.HBM) for x in tables + arrays]
    return pl.pallas_call(
        pack_kernel,
        out_shape=[pltpu.VMEM(shape, kind)] + [pltpu.VMEM(x.shape, x.dtype) for x in tables],
        in_specs=[FAR] * len(ins),
        out_specs=[WHOLE] * (1 + len(tables)),
        scratch_shapes=[
            pltpu.VMEM((len(arrays), rows, width), kind),
            pltpu.SemaphoreType.DMA((len(ins),)),
        ],
        compiler_params=pltpu.CompilerParams(vmem_limit_bytes=8 << 20),
    )(*ins)


def unpack_kernel(packed, *refs):
    outs, (held, sems) = refs[:-2], refs[-2:]
    leaving = []
    for a, out in enumerate(outs):
        for h in range(packed.shape[0]):
            held[a, :, h * HEAD_DIM : (h + 1) * HEAD_DIM] = packed[h, a]
        leaving.append(pltpu.make_async_copy(held.at[a], out, sems.at[a]))
        leaving[-1].start()
    wait_all(leaving)


def unpack(packed):
    heads, arrays, rows, depth = packed.shape
    return pl.pallas_call(
        unpack_kernel,
        out_shape=[jax.ShapeDtypeStruct((rows, heads * depth), packed.dtype)] * arrays,
        in_specs=[WHOLE],
        out_specs=[FAR] * arrays,
        scratch_shapes=[
            pltpu.VMEM((arrays, rows, heads * depth), packed.dtype),
            pltpu.SemaphoreType.DMA((arrays,)),
        ],
        compiler_params=pltpu.CompilerParams(vmem_limit_bytes=8 << 20),
    )(packed)


def place(order, lane):
    far, near = order
    team = far * near
    inside = lane % team
    return lane - inside + inside % near * far + inside // near


def tile_of(at, start, size):
    ref, slot, order = at
    rows = ref.shape[2]
    first = start // rows
    pieces = [ref[place(order, first + i), slot] for i in range(size // rows)]
    return jnp.concatenate(pieces, axis=0)


def put(at, start, tile):
    ref, slot, order = at
    rows = ref.shape[2]
    first = start // rows
    tile = tile.astype(ref.dtype)
    for i in range(tile.shape[0] // rows):
        ref[place(order, first + i), slot] = tile[i * rows : (i + 1) * rows]


def span(i, size):
    return pl.ds(pl.multiple_of(i * size, size), size)


def flip(at, out, length):
    step = min(512, length)

    def one(i, _):
        tile = tile_of(at, i * step, step)
        out[:HEAD_DIM, span(i, step)] = tile.astype(jnp.float32).T.astype(out.dtype)
        return 0

    each(length // step, one, 0)


def list_bias(random_ref, global_ref, bias_ref):
    steps, group, queries = bias_ref.shape
    blocks, total = queries // BLOCK, steps * group
    first = lax.axis_index("crew") * blocks
    shape = (blocks, total)
    names = lax.broadcasted_iota(jnp.int32, shape, 1)
    own = first + lax.broadcasted_iota(jnp.int32, shape, 0)
    times = (jnp.abs(names - own) <= 1).astype(jnp.float32)
    for i in range(global_ref.shape[1]):
        times += (names == global_ref[:, i : i + 1]).astype(jnp.float32)
    heads = random_ref.shape[2]
    head = lax.axis_index("near") * lax.axis_size("far") + lax.axis_index("far")
    mine = lax.broadcasted_iota(jnp.int32, (blocks, heads), 1) == head
    for i in range(random_ref.shape[0]):
        picks = jnp.where(mine, random_ref[i, pl.ds(first, blocks), :], 0)
        times += (names == jnp.sum(picks, axis=1, keepdims=True)).astype(jnp.float32)
    place = lax.broadcasted_iota(jnp.int32, (blocks, queries), 1) // BLOCK
    place = (place == lax.broadcasted_iota(jnp.int32, (blocks, queries), 0)).astype(jnp.bfloat16)
    wide = lax.dot_general(
        times.astype(jnp.bfloat16), place, (((0,), (0,)), ((), ())), preferred_element_type=jnp.float32
    )
    bias = jnp.where(wide > 0.0, jnp.log2(jnp.maximum(wide, 1.0)), -jnp.inf)
    bias_ref[...] = bias.reshape(steps, group, queries)


def attend_kernel(
    q_at, g_at, k_at, v_at, random_ref, global_ref, out_at, dq_at, dk_at, dv_at,
    score_ref, w_ref, ds_ref, bias_ref, kt_ref, vt_ref, gt_ref, gs_ref, delta_ref,
):
    keys, queries = w_ref.shape
    steps = keys // KEY_TILE
    turns = queries // QUERY_TILE
    factor = SCALE * math.log2(math.e)
    list_bias(random_ref, global_ref, bias_ref)
    def through(left_ref, right_ref, here):
        def add(c, total):
            at = span(c, KEY_TILE)
            return total + dot(left_ref[:, at], right_ref[at, here])

        if steps <= 4:
            return dot(left_ref[...], right_ref[:, here])
        return each(steps, add, jnp.zeros((left_ref.shape[0], QUERY_TILE), jnp.float32))

    def blocks_of(x):
        return x.reshape(KEY_TILE // BLOCK, BLOCK, QUERY_TILE)

    def score(t):
        here = span(t, QUERY_TILE)
        held = score_ref.at[t % 2]
        q = tile_of(q_at, t * QUERY_TILE, QUERY_TILE).astype(jnp.float32).T.astype(jnp.bfloat16)

        def one(c, top):
            raw = dot(tile_of(k_at, c * KEY_TILE, KEY_TILE), q)
            held[span(c, KEY_TILE), :] = raw
            listed = jnp.where(bias_ref[c, :, here] > -jnp.inf, 0.0, -jnp.inf)
            best = jnp.max(blocks_of(raw), axis=1) + listed
            return jnp.maximum(top, jnp.max(best, axis=0, keepdims=True))

        return each(steps, one, jnp.full((1, QUERY_TILE), -jnp.inf, jnp.float32)) * factor

    def weigh(t, top):
        here = span(t, QUERY_TILE)
        held = score_ref.at[t % 2]

        def one(c, _):
            at = span(c, KEY_TILE)
            shift = bias_ref[c, :, here] - top
            e = jnp.exp2(blocks_of(held[at, :]) * factor + shift[:, None, :])
            w_ref[at, here] = e.reshape(KEY_TILE, QUERY_TILE).astype(w_ref.dtype)
            return 0

        each(steps, one, 0)

    every = range(turns)
    places = [span(t, QUERY_TILE) for t in every]
    tops = [score(0)]
    flip(v_at, vt_ref, keys)
    vt_ref[HEAD_DIM:, :] = jnp.ones_like(vt_ref[HEAD_DIM:, :])
    for t in every:
        if t + 1 < turns:
            tops.append(score(t + 1))
        weigh(t, tops[t])

    grads = [tile_of(g_at, t * QUERY_TILE, QUERY_TILE).astype(jnp.float32).T for t in every]
    mixed = [through(vt_ref, w_ref, here) for here in places]
    inverse = [1.0 / x[HEAD_DIM : HEAD_DIM + 1] for x in mixed]
    outs = [(x[:HEAD_DIM] * i).astype(jnp.bfloat16) for x, i in zip(mixed, inverse)]
    scaled = [g * i for g, i in zip(grads, inverse)]
    for here, g in zip(places, scaled):
        gt_ref[:, here] = g.astype(gt_ref.dtype)
    for here, g, out in zip(places, scaled, outs):
        delta_ref[:, here] = jnp.sum(g * out.astype(jnp.float32), axis=0, keepdims=True)
    for here, g in zip(places, scaled):
        gs_ref[here, :] = g.T.astype(gs_ref.dtype)

    def values_step(c, _):
        put(dv_at, c * KEY_TILE, dot(w_ref[span(c, KEY_TILE), :], gs_ref[...]))
        return 0

    def score_grad_step(c, _):
        at = span(c, KEY_TILE)
        v = tile_of(v_at, c * KEY_TILE, KEY_TILE)
        for here in places:
            gap = dot(v, gt_ref[:, here]) - delta_ref[:, here]
            ds_ref[at, here] = (w_ref[at, here].astype(jnp.float32) * gap).astype(ds_ref.dtype)
        return 0

    def keys_step(c, _):
        q = tile_of(q_at, 0, queries)
        put(dk_at, c * KEY_TILE, dot(ds_ref[span(c, KEY_TILE), :], q) * SCALE)
        return 0

    if ds_ref is w_ref:
        each(steps, values_step, 0)
    each(steps, score_grad_step, 0)
    flip(k_at, kt_ref, keys)
    for t, out in zip(every, outs):
        put(out_at, t * QUERY_TILE, out.astype(jnp.float32).T)
    if ds_ref is not w_ref:
        each(steps, values_step, 0)
    sums = [through(kt_ref, ds_ref, here) * SCALE for here in places]
    each(steps, keys_step, 0)
    for t, dq in zip(every, sums):
        put(dq_at, t * QUERY_TILE, dq.T)


def attend(rows, wide, random_blocks, global_blocks, order):
    team, _, height, _ = rows.shape
    queries = team * height
    apart = len(wide) > 0
    keys = wide[0].shape[0] * height if apart else queries
    outs = [jax.ShapeDtypeStruct((team, 2 if apart else 4, height, HEAD_DIM), rows.dtype)]
    if apart:
        outs += [jax.ShapeDtypeStruct(x.shape, jnp.float32) for x in wide]

    def kernel(*refs):
        rows_ref, *refs = refs
        q_at, g_at, k_at, v_at = ((rows_ref, a, order) for a in range(4))
        if apart:
            k_at, v_at, *refs = [(refs[0], 0, order), (refs[1], 0, order)] + refs[2:]
        random_ref, global_ref, out_ref, *refs = refs
        out_at, dq_at, dk_at, dv_at = ((out_ref, a, order) for a in range(4))
        if apart:
            dk_at, dv_at, *refs = [(refs[0], 0, order), (refs[1], 0, order)] + refs[2:]
        score_ref, w_ref, *refs = refs
        ds_ref, *refs = [w_ref] + refs if apart else refs
        attend_kernel(
            q_at, g_at, k_at, v_at, random_ref, global_ref, out_at, dq_at, dk_at, dv_at,
            score_ref, w_ref, ds_ref, *refs,
        )

    narrow = functools.partial(pltpu.VMEM, dtype=rows.dtype)
    ins = [rows, *wide, random_blocks, global_blocks]
    return pl.pallas_call(
        kernel,
        out_shape=outs,
        in_specs=[WHOLE] * len(ins),
        out_specs=[WHOLE] * len(outs),
        scratch_shapes=[pltpu.VMEM((2, keys, QUERY_TILE), jnp.float32)]
        + [narrow((keys, queries))] * (1 if apart else 2)
        + [
            pltpu.VMEM((keys // KEY_TILE, KEY_TILE // BLOCK, queries), jnp.float32),
            narrow((HEAD_DIM, keys)),
            narrow((HEAD_DIM + 16, keys)),
            narrow((HEAD_DIM, queries)),
            narrow((queries, HEAD_DIM)),
            pltpu.VMEM((1, queries), jnp.float32),
        ],
        compiler_params=pltpu.CompilerParams(vmem_limit_bytes=(60 if apart else 24) << 20),
    )(*ins)


def body(crews, order, queries, keys, values, grad_out, random_blocks, global_blocks):
    trade = functools.partial(
        lax.all_to_all, axis_name=("near", "far"), split_axis=0, concat_axis=0, tiled=True
    )
    tables = [random_blocks.transpose(2, 1, 0), global_blocks[None, :]]
    sent, *tables = pack([queries, grad_out, keys, values], tables)
    got = trade(sent)
    wide = []
    if crews > 1:
        wide = [lax.all_gather(got[:, a : a + 1], "crew", axis=0, tiled=True) for a in (2, 3)]
    back, *sums = attend(got, wide, *tables, order)
    sums = [lax.psum_scatter(x, "crew", scatter_dimension=0, tiled=True) for x in sums]
    if crews > 1:
        back = jnp.concatenate([back] + [x.astype(back.dtype) for x in sums], axis=1)
    return tuple(unpack(trade(back)))


def solution(mesh):
    devices = mesh.devices.reshape(-1)

    def run(queries, keys, values, grad_out, random_blocks, global_blocks):
        team = queries.shape[1] // HEAD_DIM
        crews = devices.size // team
        order = (FAR_LANES, team // FAR_LANES)
        grid = Mesh(devices.reshape(crews, *order), ("crew", "far", "near"))
        split = P(("crew", "far", "near"), None)
        return jax.shard_map(
            functools.partial(body, crews, order),
            mesh=grid,
            in_specs=(split,) * 4 + (P(), P()),
            out_specs=(split,) * 4,
            check_vma=False,
        )(queries, keys, values, grad_out, random_blocks, global_blocks)

    return run
```

```python
import functools
import math

import jax
import jax.numpy as jnp
from jax import lax
from jax.experimental import pallas as pl
from jax.experimental.pallas import tpu as pltpu
from jax.sharding import Mesh
from jax.sharding import PartitionSpec as P

HEAD_DIM = 128
BLOCK = 64
SCALE = HEAD_DIM**-0.5
QUERY_TILE = 256
KEY_TILE = 256
FAR_LANES = 4

WHOLE = pl.BlockSpec(memory_space=pltpu.VMEM)
FAR = pl.BlockSpec(memory_space=pltpu.HBM)


def dot(a, b):
    return lax.dot_general(a, b, (((1,), (0,)), ((), ())), preferred_element_type=jnp.float32)


def each(count, step, start):
    if count <= 4:
        carry = start
        for i in range(count):
            carry = step(i, carry)
        return carry
    return lax.fori_loop(0, count, step, start)


def copies(pairs, sems):
    made = [pltpu.make_async_copy(a, b, sems.at[i]) for i, (a, b) in enumerate(pairs)]
    for copy in made:
        copy.start()
    return made


def wait_all(made):
    for copy in made:
        copy.wait()


def pack_kernel(random_ref, global_ref, *refs):
    *ins, out, random_out, global_out, held, sems = refs
    pairs = [(x, held.at[a]) for a, x in enumerate(ins)]
    pairs += [(random_ref, random_out), (global_ref, global_out)]
    arriving = copies(pairs, sems)
    for a in range(len(ins)):
        arriving[a].wait()
        for h in range(out.shape[0]):
            out[h, a] = held[a, :, h * HEAD_DIM : (h + 1) * HEAD_DIM]
    wait_all(arriving[len(ins) :])


def pack(arrays, tables):
    rows, width = arrays[0].shape
    kind = arrays[0].dtype
    shape = (width // HEAD_DIM, len(arrays), rows, HEAD_DIM)
    ins = [pltpu.with_memory_space_constraint(x, pltpu.HBM) for x in tables + arrays]
    return pl.pallas_call(
        pack_kernel,
        out_shape=[pltpu.VMEM(shape, kind)] + [pltpu.VMEM(x.shape, x.dtype) for x in tables],
        in_specs=[FAR] * len(ins),
        out_specs=[WHOLE] * (1 + len(tables)),
        scratch_shapes=[
            pltpu.VMEM((len(arrays), rows, width), kind),
            pltpu.SemaphoreType.DMA((len(ins),)),
        ],
        compiler_params=pltpu.CompilerParams(vmem_limit_bytes=8 << 20),
    )(*ins)


def unpack_kernel(packed, *refs):
    outs, (held, sems) = refs[:-2], refs[-2:]
    leaving = []
    for a, out in enumerate(outs):
        for h in range(packed.shape[0]):
            held[a, :, h * HEAD_DIM : (h + 1) * HEAD_DIM] = packed[h, a]
        leaving.append(pltpu.make_async_copy(held.at[a], out, sems.at[a]))
        leaving[-1].start()
    wait_all(leaving)


def unpack(packed):
    heads, arrays, rows, depth = packed.shape
    return pl.pallas_call(
        unpack_kernel,
        out_shape=[jax.ShapeDtypeStruct((rows, heads * depth), packed.dtype)] * arrays,
        in_specs=[WHOLE],
        out_specs=[FAR] * arrays,
        scratch_shapes=[
            pltpu.VMEM((arrays, rows, heads * depth), packed.dtype),
            pltpu.SemaphoreType.DMA((arrays,)),
        ],
        compiler_params=pltpu.CompilerParams(vmem_limit_bytes=8 << 20),
    )(packed)


def place(order, lane):
    far, near = order
    team = far * near
    inside = lane % team
    return lane - inside + inside % near * far + inside // near


def tile_of(at, start, size):
    ref, slot, order = at
    rows = ref.shape[2]
    first = start // rows
    pieces = [ref[place(order, first + i), slot] for i in range(size // rows)]
    return jnp.concatenate(pieces, axis=0)


def put(at, start, tile):
    ref, slot, order = at
    rows = ref.shape[2]
    first = start // rows
    tile = tile.astype(ref.dtype)
    for i in range(tile.shape[0] // rows):
        ref[place(order, first + i), slot] = tile[i * rows : (i + 1) * rows]


def span(i, size):
    return pl.ds(pl.multiple_of(i * size, size), size)


def flip(at, out, length):
    step = min(512, length)

    def one(i, _):
        tile = tile_of(at, i * step, step)
        out[:HEAD_DIM, span(i, step)] = tile.astype(jnp.float32).T.astype(out.dtype)
        return 0

    each(length // step, one, 0)


def list_bias(random_ref, global_ref, bias_ref):
    steps, group, queries = bias_ref.shape
    blocks, total = queries // BLOCK, steps * group
    first = lax.axis_index("crew") * blocks
    shape = (blocks, total)
    names = lax.broadcasted_iota(jnp.int32, shape, 1)
    own = first + lax.broadcasted_iota(jnp.int32, shape, 0)
    times = (jnp.abs(names - own) <= 1).astype(jnp.float32)
    for i in range(global_ref.shape[1]):
        times += (names == global_ref[:, i : i + 1]).astype(jnp.float32)
    heads = random_ref.shape[2]
    head = lax.axis_index("near") * lax.axis_size("far") + lax.axis_index("far")
    mine = lax.broadcasted_iota(jnp.int32, (blocks, heads), 1) == head
    for i in range(random_ref.shape[0]):
        picks = jnp.where(mine, random_ref[i, pl.ds(first, blocks), :], 0)
        times += (names == jnp.sum(picks, axis=1, keepdims=True)).astype(jnp.float32)
    place = lax.broadcasted_iota(jnp.int32, (blocks, queries), 1) // BLOCK
    place = (place == lax.broadcasted_iota(jnp.int32, (blocks, queries), 0)).astype(jnp.bfloat16)
    wide = lax.dot_general(
        times.astype(jnp.bfloat16), place, (((0,), (0,)), ((), ())), preferred_element_type=jnp.float32
    )
    bias = jnp.where(wide > 0.0, jnp.log2(jnp.maximum(wide, 1.0)), -jnp.inf)
    bias_ref[...] = bias.reshape(steps, group, queries)


def attend_kernel(
    q_at, g_at, k_at, v_at, random_ref, global_ref, out_at, dq_at, dk_at, dv_at,
    score_ref, w_ref, ds_ref, bias_ref, kt_ref, vt_ref, gt_ref, gs_ref, delta_ref,
):
    keys, queries = w_ref.shape
    steps = keys // KEY_TILE
    turns = queries // QUERY_TILE
    factor = SCALE * math.log2(math.e)
    list_bias(random_ref, global_ref, bias_ref)
    flip(v_at, vt_ref, keys)
    vt_ref[HEAD_DIM:, :] = jnp.ones_like(vt_ref[HEAD_DIM:, :])

    def through(left_ref, right_ref, here):
        def add(c, total):
            at = span(c, KEY_TILE)
            return total + dot(left_ref[:, at], right_ref[at, here])

        if steps <= 4:
            return dot(left_ref[...], right_ref[:, here])
        return each(steps, add, jnp.zeros((left_ref.shape[0], QUERY_TILE), jnp.float32))

    def blocks_of(x):
        return x.reshape(KEY_TILE // BLOCK, BLOCK, QUERY_TILE)

    def score(t):
        here = span(t, QUERY_TILE)
        held = score_ref.at[t % 2]
        q = tile_of(q_at, t * QUERY_TILE, QUERY_TILE).astype(jnp.float32).T.astype(jnp.bfloat16)

        def one(c, top):
            raw = dot(tile_of(k_at, c * KEY_TILE, KEY_TILE), q)
            held[span(c, KEY_TILE), :] = raw
            listed = jnp.where(bias_ref[c, :, here] > -jnp.inf, 0.0, -jnp.inf)
            best = jnp.max(blocks_of(raw), axis=1) + listed
            return jnp.maximum(top, jnp.max(best, axis=0, keepdims=True))

        return each(steps, one, jnp.full((1, QUERY_TILE), -jnp.inf, jnp.float32)) * factor

    def weigh(t, top):
        here = span(t, QUERY_TILE)
        held = score_ref.at[t % 2]

        def one(c, _):
            at = span(c, KEY_TILE)
            shift = bias_ref[c, :, here] - top
            e = jnp.exp2(blocks_of(held[at, :]) * factor + shift[:, None, :])
            w_ref[at, here] = e.reshape(KEY_TILE, QUERY_TILE).astype(w_ref.dtype)
            return 0

        each(steps, one, 0)

    def mix(t):
        here = span(t, QUERY_TILE)
        mixed = through(vt_ref, w_ref, here)
        inverse = 1.0 / mixed[HEAD_DIM : HEAD_DIM + 1]
        out = (mixed[:HEAD_DIM] * inverse).astype(jnp.bfloat16).astype(jnp.float32)
        put(out_at, t * QUERY_TILE, out.T)
        g = tile_of(g_at, t * QUERY_TILE, QUERY_TILE).astype(jnp.float32).T
        delta_ref[:, here] = jnp.sum(g * out, axis=0, keepdims=True) * inverse
        g = g * inverse
        gt_ref[:, here] = g.astype(gt_ref.dtype)
        gs_ref[here, :] = g.T.astype(gs_ref.dtype)

    tops = [score(0)]
    for t in range(turns):
        if t + 1 < turns:
            tops.append(score(t + 1))
        weigh(t, tops[t])
        mix(t)

    def backward(c, _):
        at = span(c, KEY_TILE)
        put(dv_at, c * KEY_TILE, dot(w_ref[at, :], gs_ref[...]))
        v = tile_of(v_at, c * KEY_TILE, KEY_TILE)
        for t in range(turns):
            here = span(t, QUERY_TILE)
            gap = dot(v, gt_ref[:, here]) - delta_ref[:, here]
            ds_ref[at, here] = (w_ref[at, here].astype(jnp.float32) * gap).astype(ds_ref.dtype)
        q = tile_of(q_at, 0, queries)
        put(dk_at, c * KEY_TILE, dot(ds_ref[at, :], q) * SCALE)
        return 0

    each(steps, backward, 0)
    flip(k_at, kt_ref, keys)
    for t in range(turns):
        put(dq_at, t * QUERY_TILE, (through(kt_ref, ds_ref, span(t, QUERY_TILE)) * SCALE).T)


def attend(rows, wide, random_blocks, global_blocks, order):
    team, _, height, _ = rows.shape
    queries = team * height
    apart = len(wide) > 0
    keys = wide[0].shape[0] * height if apart else queries
    outs = [jax.ShapeDtypeStruct((team, 2 if apart else 4, height, HEAD_DIM), rows.dtype)]
    if apart:
        outs += [jax.ShapeDtypeStruct(x.shape, jnp.float32) for x in wide]

    def kernel(*refs):
        rows_ref, *refs = refs
        q_at, g_at, k_at, v_at = ((rows_ref, a, order) for a in range(4))
        if apart:
            k_at, v_at, *refs = [(refs[0], 0, order), (refs[1], 0, order)] + refs[2:]
        random_ref, global_ref, out_ref, *refs = refs
        out_at, dq_at, dk_at, dv_at = ((out_ref, a, order) for a in range(4))
        if apart:
            dk_at, dv_at, *refs = [(refs[0], 0, order), (refs[1], 0, order)] + refs[2:]
        score_ref, w_ref, *refs = refs
        ds_ref, *refs = [w_ref] + refs if apart else refs
        attend_kernel(
            q_at, g_at, k_at, v_at, random_ref, global_ref, out_at, dq_at, dk_at, dv_at,
            score_ref, w_ref, ds_ref, *refs,
        )

    narrow = functools.partial(pltpu.VMEM, dtype=rows.dtype)
    ins = [rows, *wide, random_blocks, global_blocks]
    return pl.pallas_call(
        kernel,
        out_shape=outs,
        in_specs=[WHOLE] * len(ins),
        out_specs=[WHOLE] * len(outs),
        scratch_shapes=[pltpu.VMEM((2, keys, QUERY_TILE), jnp.float32)]
        + [narrow((keys, queries))] * (1 if apart else 2)
        + [
            pltpu.VMEM((keys // KEY_TILE, KEY_TILE // BLOCK, queries), jnp.float32),
            narrow((HEAD_DIM, keys)),
            narrow((HEAD_DIM + 16, keys)),
            narrow((HEAD_DIM, queries)),
            narrow((queries, HEAD_DIM)),
            pltpu.VMEM((1, queries), jnp.float32),
        ],
        compiler_params=pltpu.CompilerParams(vmem_limit_bytes=(60 if apart else 24) << 20),
    )(*ins)


def body(crews, order, queries, keys, values, grad_out, random_blocks, global_blocks):
    trade = functools.partial(
        lax.all_to_all, axis_name=("near", "far"), split_axis=0, concat_axis=0, tiled=True
    )
    tables = [random_blocks.transpose(2, 1, 0), global_blocks[None, :]]
    sent, *tables = pack([queries, grad_out, keys, values], tables)
    got = trade(sent)
    wide = []
    if crews > 1:
        wide = [lax.all_gather(got[:, a : a + 1], "crew", axis=0, tiled=True) for a in (2, 3)]
    back, *sums = attend(got, wide, *tables, order)
    sums = [lax.psum_scatter(x, "crew", scatter_dimension=0, tiled=True) for x in sums]
    if crews > 1:
        back = jnp.concatenate([back] + [x.astype(back.dtype) for x in sums], axis=1)
    return tuple(unpack(trade(back)))


def solution(mesh):
    devices = mesh.devices.reshape(-1)

    def run(queries, keys, values, grad_out, random_blocks, global_blocks):
        team = queries.shape[1] // HEAD_DIM
        crews = devices.size // team
        order = (FAR_LANES, team // FAR_LANES)
        grid = Mesh(devices.reshape(crews, *order), ("crew", "far", "near"))
        split = P(("crew", "far", "near"), None)
        return jax.shard_map(
            functools.partial(body, crews, order),
            mesh=grid,
            in_specs=(split,) * 4 + (P(), P()),
            out_specs=(split,) * 4,
            check_vma=False,
        )(queries, keys, values, grad_out, random_blocks, global_blocks)

    return run
```
